512 devices in a mesh: pipe: 32 (over x, z_lo), dp: 2 (over z_hi), tensor: 8 (over y, core).
Axes of the slice: x: 4, y: 4, z: 16 (z_hi: 2, z_lo: 8; z = z_hi * 8 + z_lo), core: 2. Of those that a mesh axis runs over, the one named last changes fastest.
Arguments:
- acts_in: bfloat16 [32, 2, 2, 96, 2048], P('pipe', 'dp', None, 'tensor'), may hold values from -6 to 6
- saved_in: bfloat16 [32, 2, 2, 96, 2048], P('pipe', 'dp', None, 'tensor'), may hold values from -6 to 6
- out_grad: bfloat16 [32, 2, 2, 96, 2048], P('pipe', 'dp', None, 'tensor'), may hold values from -1.5 to 1.5
- w_query: bfloat16 [32, 2048, 2048], P('pipe', None, 'tensor'), may hold values from -0.125 to 0.125
- w_keyval: bfloat16 [32, 2048, 2, 1024], P('pipe', None, None, 'tensor'), may hold values from -0.125 to 0.125
- w_out: bfloat16 [32, 2048, 2048], P('pipe', 'tensor'), may hold values from -0.125 to 0.125
- kept_rows: int32 [32, 2, 2, 96], P('pipe', 'dp'), may hold values from 0 to 191, as said below
- doc_lengths: int32 [32, 2, 2, 4], P('pipe', 'dp'), may hold values from 1 to 96, 192 in all within a row
Outputs:
- handed: bfloat16 [32, 2, 2, 96, 2048], P('pipe', 'dp', None, 'tensor')
- back: bfloat16 [32, 2, 2, 96, 2048], P('pipe', 'dp', None, 'tensor')
- grad_query: bfloat16 [32, 2048, 2048], P('pipe', 'dp', 'tensor')
- grad_keyval: bfloat16 [32, 2048, 2, 1024], P('pipe', 'dp', None, 'tensor')
- grad_out: bfloat16 [32, 2048, 2048], P('pipe', 'tensor', 'dp')
The draws below stay inside these ranges and needn't reach their ends.
Inputs may be any that keep to these rules, and one draw needn't show every extreme that they name: `kept_rows`: each list names 96 distinct rows in increasing order. `doc_lengths`: a list's 4 lengths sum to 192.
All inputs are finite; a program needn't handle non-finite values.
Results may differ from the reference program's by a relative error of at most 0.015.
Values may be sent and summed in bfloat16 or wider, within the bound.
A program may use at most 64 MiB of HBM per device.

```python
import math
import jax
import jax.numpy as jnp
import numpy as np
from jax import lax

D = 2048
HEADS = 16
KV_HEADS = 8
HEAD = 128
ROWS = 192
DOCS = 4
KEEP = 96
N_PIPE = 32
N_DP = 2


def draw_kept_rows(key, part):
    key = jax.random.fold_in(key, 11)
    row_keys = jax.random.split(key, N_PIPE * N_DP * 2)
    shuffled = jax.vmap(lambda entry: jax.random.permutation(entry, ROWS))(row_keys)
    chosen = jnp.sort(shuffled[:, :KEEP], axis=1)
    return chosen.reshape(N_PIPE, N_DP, 2, KEEP).astype(jnp.int32)


def level_of(own_key, dims, shards, smallest, high):
    gain, own = 1.0, jax.random.fold_in(own_key, 6)
    for dim, shards_of in shards:
        heights = jnp.exp(jax.random.uniform(jax.random.fold_in(own, dim), (shards_of,), jnp.float32, smallest / len(shards), high / len(shards)))
        gain = gain * jnp.repeat(heights, dims[dim] // shards_of).reshape([-1 if axis == dim else 1 for axis in range(len(dims))])
    return gain


def profile(count, total, limit, lean):
    loads = [(1 << 20) // math.isqrt(grade ** lean) + 1 for grade in range(2, count + 1)]
    rest, counts = total - limit - (count - 1), [1] * (count - 1)
    while rest > 0:
        movable = [i for i in range(count - 1) if counts[i] < limit]
        whole, left = sum([loads[i] for i in movable]), rest
        for i in movable:
            more = min(limit - counts[i], max(1, left * loads[i] // whole), rest)
            counts[i] = counts[i] + more
            rest = rest - more
    return np.array([limit] + counts)


def uneven(own_key, amount, total, most, lean):
    if amount == 2:
        one = jax.random.randint(own_key, (), max(1, total - most), min(most, total - 1) + 1)
        return jnp.stack([one, total - one])
    sizes = jnp.asarray(profile(amount, total, most, lean), jnp.int32)
    couples = (amount - 1) // 2
    donor, taker = sizes[1:1 + 2 * couples:2], sizes[2:2 + 2 * couples:2]
    room = jnp.minimum(donor - 1, most - taker)
    moved = jax.random.randint(jax.random.fold_in(own_key, 1), (couples,), 0, 1 << 20) % (room + 1)
    sizes = sizes.at[1:1 + 2 * couples:2].set(donor - moved).at[2:2 + 2 * couples:2].set(taker + moved)
    return sizes[jax.random.permutation(jax.random.fold_in(own_key, 2), amount)]


def scatter_about(rng, shape, deviation, most, cuts=(), held_as=jnp.bfloat16):
    values = deviation * jax.random.normal(rng, shape, jnp.float32)
    if cuts:
        values = values * level_of(rng, shape, cuts, -0.22, 0.18)
    return jnp.clip(values, -most, most).astype(held_as)


def setup_inputs(seed: int = 0) -> dict:
    seeds = jax.random.split(jax.random.key(seed), 9)
    acts_in = scatter_about(seeds[0], (N_PIPE, N_DP, 2, KEEP, D), 1.0, 6.0, ((0, 32), (1, 2), (3, 8)))
    saved_in = scatter_about(seeds[1], (N_PIPE, N_DP, 2, KEEP, D), 1.0, 6.0, ((0, 32), (1, 2), (3, 8)))
    out_grad = scatter_about(seeds[2], (N_PIPE, N_DP, 2, KEEP, D), 0.25, 1.5, ((0, 32), (1, 2), (3, 8)))
    w_query = scatter_about(seeds[3], (N_PIPE, D, HEADS * HEAD), D ** -0.5, 0.125, ((0, 32), (2, 8)))
    w_keyval = scatter_about(seeds[4], (N_PIPE, D, 2, KV_HEADS * HEAD), D ** -0.5, 0.125, ((0, 32), (3, 8)))
    w_out = scatter_about(seeds[5], (N_PIPE, HEADS * HEAD, D), (HEADS * HEAD) ** -0.5, 0.125, ((0, 32), (1, 8)))
    kept_rows = draw_kept_rows(jax.random.fold_in(seeds[8], 71), 0)
    doc_lengths = jax.vmap(lambda own: uneven(own, DOCS, ROWS, KEEP, 1))(jax.random.split(seeds[7], N_PIPE * N_DP * 2)).reshape((N_PIPE, N_DP, 2, DOCS)).astype(jnp.int32)
    return {"acts_in": acts_in, "saved_in": saved_in, "out_grad": out_grad, "w_query": w_query, "w_keyval": w_keyval, "w_out": w_out, "kept_rows": kept_rows, "doc_lengths": doc_lengths}


EPSILON = 1e-06

def rounded(values):
    return lax.optimization_barrier(values.astype(jnp.bfloat16)).astype(jnp.float32)

def norm_rows(rows_in):
    widened = rows_in.astype(jnp.float32)
    inv_scale = lax.rsqrt(lax.optimization_barrier(jnp.mean(widened * widened, axis=1, keepdims=True)) + EPSILON)
    return (widened * inv_scale, inv_scale)

def doc_numbers(lengths, row_ids):
    bounds = jnp.cumsum(lengths)
    return lax.optimization_barrier(jnp.sum((row_ids[:, None] >= bounds[None, :]).astype(jnp.int32), axis=1))

def arrange(kept_list, row_ids):
    kept_flags = jnp.any(kept_list[None, :] == row_ids[:, None], axis=1).astype(jnp.int32)
    row_order = jnp.argsort(1 - kept_flags, stable=True).astype(jnp.int32)
    inverse = jnp.argsort(row_order, stable=True).astype(jnp.int32)
    return (row_order, inverse)

def heads_forward(rows_in, positions, documents, query_weight, keyval_weight):
    row_count = rows_in.shape[0]
    unrounded, inv_scale = norm_rows(rows_in)
    normed = unrounded.astype(jnp.bfloat16)
    flat_keyval = keyval_weight.reshape(keyval_weight.shape[0], -1)
    queries = rounded(jnp.dot(normed, query_weight, preferred_element_type=jnp.float32))
    keyval = rounded(jnp.dot(normed, flat_keyval, preferred_element_type=jnp.float32))
    groups = flat_keyval.shape[1] // (2 * HEAD)
    split_at = groups * HEAD
    queries = queries.reshape(row_count, groups, -1, HEAD)
    key_heads = keyval[:, :split_at].reshape(row_count, groups, HEAD)
    value_heads = keyval[:, split_at:].reshape(row_count, groups, HEAD)
    scores = jnp.einsum('qgcd,kgd->gcqk', queries, key_heads) * HEAD ** (-0.5)
    allowed = (documents[:, None] == documents[None, :]) & (positions[None, :] <= positions[:, None])
    probabilities = jax.nn.softmax(jnp.where(allowed, scores, -jnp.inf), axis=-1)
    rounded_probs = rounded(probabilities)
    mixed_heads = jnp.einsum('gcqk,kgd->qgcd', rounded_probs, value_heads)
    mixed_heads = mixed_heads.reshape(row_count, -1).astype(jnp.bfloat16)
    return (normed, queries, key_heads, value_heads, probabilities, rounded_probs, mixed_heads)

def layer_forward(rows_in, positions, documents, query_weight, keyval_weight, out_weight):
    mixed_heads = heads_forward(rows_in, positions, documents, query_weight, keyval_weight)[-1]
    attended = jnp.dot(mixed_heads, out_weight, preferred_element_type=jnp.float32)
    return (rows_in.astype(jnp.float32) + attended).astype(jnp.bfloat16)

def layer_backward(rows_in, upstream, positions, documents, query_weight, keyval_weight, out_weight):
    normed, queries, key_heads, value_heads, probabilities, rounded_probs, mixed_heads = heads_forward(rows_in, positions, documents, query_weight, keyval_weight)
    row_count = rows_in.shape[0]
    flat_keyval = keyval_weight.reshape(keyval_weight.shape[0], -1)
    grad_mixed = rounded(jnp.dot(upstream, out_weight.T, preferred_element_type=jnp.float32))
    grad_mixed = grad_mixed.reshape(queries.shape)
    grad_probs = jnp.einsum('qgcd,kgd->gcqk', grad_mixed, value_heads)
    centre = lax.optimization_barrier(jnp.sum(probabilities * grad_probs, axis=-1, keepdims=True))
    grad_scores = rounded(probabilities * (grad_probs - centre) * HEAD ** (-0.5))
    grad_query = jnp.einsum('gcqk,kgd->qgcd', grad_scores, key_heads).reshape(row_count, -1).astype(jnp.bfloat16)
    grad_keys = jnp.einsum('gcqk,qgcd->kgd', grad_scores, queries).reshape(row_count, -1).astype(jnp.bfloat16)
    grad_values = jnp.einsum('gcqk,qgcd->kgd', rounded_probs, grad_mixed).reshape(row_count, -1).astype(jnp.bfloat16)
    grad_keyval = jnp.concatenate([grad_keys, grad_values], axis=1)
    grad_normed = jnp.dot(grad_query, query_weight.T, preferred_element_type=jnp.float32)
    grad_normed = grad_normed + jnp.dot(grad_keyval, flat_keyval.T, preferred_element_type=jnp.float32)
    unrounded, inv_scale = norm_rows(rows_in)
    inner_mean = lax.optimization_barrier(jnp.mean(grad_normed * unrounded, axis=1, keepdims=True))
    grad_rows = (upstream.astype(jnp.float32) + inv_scale * (grad_normed - unrounded * inner_mean)).astype(jnp.bfloat16)
    weight_grads = (jnp.dot(normed.T, grad_query, preferred_element_type=jnp.float32), jnp.dot(normed.T, grad_keyval, preferred_element_type=jnp.float32).reshape(normed.shape[1], 2, -1), jnp.dot(mixed_heads.T, upstream, preferred_element_type=jnp.float32))
    return (grad_rows, weight_grads)

def reference(acts_in, saved_in, out_grad, w_query, w_keyval, w_out, kept_rows, doc_lengths):
    span_first = 0
    span_last = N_PIPE - 1
    row_ids = jnp.arange(ROWS, dtype=jnp.int32)
    empty_rows = jnp.zeros((KEEP, D), jnp.bfloat16)
    section_outputs = []
    section_backs = []
    grad_lists = ([], [], [])
    skip_forward = []
    skip_backward = []
    for section_id in range(N_PIPE):
        query_weight = w_query[section_id]
        keyval_weight = w_keyval[section_id]
        out_weight = w_out[section_id]
        outputs_here = []
        backs_here = []
        grads_here = []
        for replica in range(N_DP):
            buffer = acts_in[section_id, replica]
            straight = buffer.reshape(ROWS, D)
            kept_list = kept_rows[section_id, replica, 0]
            documents = doc_numbers(doc_lengths[section_id, replica, 0], row_ids)
            row_order, inverse = arrange(kept_list, row_ids)
            if section_id < span_first or section_id > span_last:
                result = layer_forward(straight, row_ids, documents, query_weight, keyval_weight, out_weight)
                result = result.reshape(2, KEEP, D)
            elif section_id == span_first:
                picked = layer_forward(straight[kept_list], kept_list, documents[kept_list], query_weight, keyval_weight, out_weight)
                result = jnp.stack([picked, empty_rows])
                skip_forward.append(straight[row_order[KEEP:]])
            elif section_id < span_last:
                picked = layer_forward(buffer[0], kept_list, documents[kept_list], query_weight, keyval_weight, out_weight)
                result = jnp.stack([picked, empty_rows])
            else:
                result = layer_forward(straight[inverse], row_ids, documents, query_weight, keyval_weight, out_weight)
                result = result.reshape(2, KEEP, D)
            outputs_here.append(result)
            saved = saved_in[section_id, replica]
            saved_straight = saved.reshape(ROWS, D)
            upstream = out_grad[section_id, replica]
            kept_back = kept_rows[section_id, replica, 1]
            docs_back = doc_numbers(doc_lengths[section_id, replica, 1], row_ids)
            order_back, inverse_back = arrange(kept_back, row_ids)
            if section_id < span_first or section_id > span_last:
                grad_rows, weight_grads = layer_backward(saved_straight, upstream.reshape(ROWS, D), row_ids, docs_back, query_weight, keyval_weight, out_weight)
                back_buffer = grad_rows.reshape(2, KEEP, D)
            elif section_id == span_first:
                grad_kept, weight_grads = layer_backward(saved_straight[kept_back], upstream[0], kept_back, docs_back[kept_back], query_weight, keyval_weight, out_weight)
                joined = jnp.concatenate([grad_kept, upstream[1]], axis=0)[inverse_back]
                back_buffer = joined.reshape(2, KEEP, D)
            elif section_id < span_last:
                grad_kept, weight_grads = layer_backward(saved[0], upstream[0], kept_back, docs_back[kept_back], query_weight, keyval_weight, out_weight)
                back_buffer = jnp.stack([grad_kept, empty_rows])
            else:
                grad_rows, weight_grads = layer_backward(saved_straight[inverse_back], upstream.reshape(ROWS, D), row_ids, docs_back, query_weight, keyval_weight, out_weight)
                back_buffer = jnp.stack([grad_rows[kept_back], empty_rows])
                skip_backward.append(grad_rows[order_back[KEEP:]])
            backs_here.append(back_buffer)
            grads_here.append(weight_grads)
        section_outputs.append(jnp.stack(outputs_here))
        section_backs.append(jnp.stack(backs_here))
        for which in range(3):
            accumulated = rounded(grads_here[0][which])
            for replica in range(1, N_DP):
                accumulated = accumulated + rounded(grads_here[replica][which])
            grad_lists[which].append(accumulated.astype(jnp.bfloat16))
    zero_block = jnp.zeros((N_DP, 2, KEEP, D), jnp.bfloat16)
    handed = [zero_block] + section_outputs[:-1]
    handed[span_last] = jnp.stack([handed[span_last][:, 0], jnp.stack(skip_forward)], axis=1)
    returned = section_backs[1:] + [zero_block]
    returned[span_first] = jnp.stack([returned[span_first][:, 0], jnp.stack(skip_backward)], axis=1)
    return (jnp.stack(handed), jnp.stack(returned), jnp.stack(grad_lists[0]), jnp.stack(grad_lists[1]), jnp.stack(grad_lists[2]))
```

```python
import jax
import jax.numpy as jnp
from jax import lax
from jax.experimental import pallas as pl
from jax.experimental.pallas import tpu as pltpu
from jax.sharding import PartitionSpec as P

HEAD = 128
EPSILON = 1e-06
MESH = pl.DeviceIdType.MESH
F32 = jnp.float32
BF16 = jnp.bfloat16

SAVED, GRAD, ACTS, SAVED_2, GRAD_2 = range(5)
BACK, FORWARD = 0, 1
ROWS_PAD = 16
SLABS = 8
HALF_ROWS = SLABS * ROWS_PAD


def nn(a, b):
    return lax.dot_general(a, b, (((1,), (0,)), ((), ())), preferred_element_type=F32)


def nt(a, b):
    return lax.dot_general(a, b, (((1,), (1,)), ((), ())), preferred_element_type=F32)


def tn(a, b):
    return lax.dot_general(a, b, (((0,), (0,)), ((), ())), preferred_element_type=F32)


def iota(shape, dim):
    return lax.broadcasted_iota(jnp.int32, shape, dim)


def list_index(a, real_rows):
    core, y, r = a // 64, (a // 16) % 4, a % 16
    return (2 * y + core) * real_rows + r, r < real_rows


def to_row(col):
    n = col.shape[0]
    return jnp.sum(jnp.where(iota((n, n), 0) == iota((n, n), 1), col, 0.0), axis=0, keepdims=True)


def to_col(row):
    n = row.shape[1]
    return jnp.sum(jnp.where(iota((n, n), 0) == iota((n, n), 1), row, 0.0), axis=1, keepdims=True)


def kept_positions(kept, real_rows):
    keep = kept.shape[1]
    place, real = list_index(iota((HALF_ROWS, keep), 0), real_rows)
    hit = (place == iota((HALF_ROWS, keep), 1)) & real
    found = jnp.sum(jnp.where(hit, kept, 0.0), axis=1, keepdims=True)
    _, real_col = list_index(iota((HALF_ROWS, 1), 0), real_rows)
    return jnp.where(real_col, found, 1000.0)


def dropped_positions(kept, real_rows):
    keep = kept.shape[1]
    n = 256
    named = jnp.max(
        jnp.where(iota((n, keep), 0).astype(F32) == kept, 1.0, 0.0), axis=1, keepdims=True
    )
    free = jnp.where(iota((n, 1), 0) < 2 * keep, 1.0 - named, 0.0)
    count = jnp.sum(
        jnp.where(iota((n, n), 1) <= iota((n, n), 0), to_row(free), 0.0), axis=1, keepdims=True
    )
    place, real = list_index(iota((n, HALF_ROWS), 1), real_rows)
    hit = (count - 1.0 == place.astype(F32)) & (free > 0.5) & real
    found = jnp.sum(jnp.where(hit, iota((n, HALF_ROWS), 0).astype(F32), 0.0), axis=0, keepdims=True)
    _, real_row = list_index(iota((1, HALF_ROWS), 1), real_rows)
    return jnp.where(real_row, found, 1000.0)


def document_of(positions, lengths):
    bound = jnp.zeros((1, 1), F32)
    total = jnp.zeros(positions.shape, F32)
    for m in range(lengths.shape[1]):
        bound = bound + lengths[:, m : m + 1]
        total = total + jnp.where(positions >= bound, 1.0, 0.0)
    return total


def select(pos_col, real_rows, keep):
    n = 2 * HALF_ROWS
    b = iota((1, n), 1)
    place, real = list_index(b % HALF_ROWS, real_rows)
    flat = jnp.where(real, (b // HALF_ROWS) * keep + place, -1).astype(F32)
    return jnp.where(pos_col == flat, 1.0, 0.0).astype(BF16)


def inverse_root(x):
    return lax.rsqrt(jnp.mean(x * x, axis=1, keepdims=True) + EPSILON)


def kernel(
    acts, saved, ograd, kept, lens, wq_hbm, wkv_hbm, wo_hbm,
    handed, back, gq_out, gkv_out, go_out,
    buf, wq, wkv, wo, kept2, lens2, normed, picked, gpick, stash, part, sibrecv, chip, yrecv, hsrc, hrecv,
    wsem, dps, dpr, ags, agr, r1s, r1r, r2s, r2r, hs, hr,
):
    pipes = lax.axis_size("pipe")
    p, r, t = lax.axis_index("pipe"), lax.axis_index("dp"), lax.axis_index("tensor")
    y, c = t // 2, t % 2
    own = c * 4 + y
    first, last = p == 0, p == pipes - 1
    edge = first | last
    inner = jnp.logical_not(edge)
    real_rows, width = acts.shape[3], acts.shape[4]
    keep = kept.shape[3]
    half_width = width // 2
    next_pipe = {"pipe": lax.rem(p + 1, pipes)}
    prev_pipe = {"pipe": lax.rem(p + pipes - 1, pipes)}
    sibling = {"tensor": y * 2 + 1 - c}
    other_dp = {"dp": 1 - r}

    def peer_y(d):
        return lax.rem(y + d, 4)

    def remote(src, dst, send, recv, device):
        return pltpu.make_async_remote_copy(
            src_ref=src, dst_ref=dst, send_sem=send, recv_sem=recv, device_id=device, device_id_type=MESH
        )

    def slots_of(arr, action):
        action(arr, 0)
        used = last if arr in (GRAD, GRAD_2) else edge

        @pl.when(used)
        def _():
            action(arr, 1)

    loads = [
        pltpu.make_async_copy(src.at[0] if src is not wkv_hbm else src, dst, wsem.at[i])
        for i, (src, dst) in enumerate(((wq_hbm, wq), (wkv_hbm, wkv), (wo_hbm, wo)))
    ]
    for load in loads:
        load.start()

    barrier = pltpu.get_barrier_semaphore()
    greet = [{"tensor": lax.rem(t + d, 8)} for d in range(1, 8)] + [other_dp, next_pipe, prev_pipe]
    for device in greet:
        pl.semaphore_signal(barrier, inc=1, device_id=device, device_id_type=MESH)

    filler = jnp.zeros((ROWS_PAD - real_rows, width), BF16)
    for arr, src in ((SAVED, saved), (GRAD, ograd), (ACTS, acts)):
        for slot in range(2):
            buf[arr, slot, own, 0:real_rows, :] = src[0, 0, slot]
            buf[arr, slot, own, real_rows:, :] = filler

    pl.semaphore_wait(barrier, len(greet))

    def dp_copy(arr, slot):
        return remote(
            buf.at[arr, slot, own], buf.at[arr + 3, slot, own],
            dps.at[arr, slot], dpr.at[arr, slot], other_dp,
        )

    kept_copy = remote(kept.at[0, 0], kept2, dps.at[2, 0], dpr.at[2, 0], other_dp)
    lens_copy = remote(lens.at[0, 0], lens2, dps.at[2, 1], dpr.at[2, 1], other_dp)
    slots_of(SAVED, lambda arr, slot: dp_copy(arr, slot).start())
    slots_of(GRAD, lambda arr, slot: dp_copy(arr, slot).start())
    kept_copy.start()
    lens_copy.start()

    def slab_to(arr, slot, slab, sem, device):
        here = buf.at[arr, slot, slab]
        return remote(here, here, ags.at[arr, slot, sem], agr.at[arr, slot, slab], device)

    def ag_start(arr, slot):
        for d in (2, 1, 3):
            slab_to(arr, slot, own, d - 1, {"tensor": peer_y(d) * 2 + c}).start()
        slab_to(arr, slot, own, 3, sibling).start()

    def ag_pass(arr, slot):
        for d in (1, 3, 2):
            slab = c * 4 + peer_y(d)
            copy = slab_to(arr, slot, slab, 3 + d, sibling)
            copy.wait_recv()
            copy.start()

    def ag_wait(arr, slot):
        for d in range(4):
            slab_to(arr, slot, (1 - c) * 4 + peer_y(d), 3, sibling).wait_recv()

    def ag_end(arr, slot):
        for d in range(7):
            slab_to(arr, slot, own, d, sibling).wait_send()

    for arr in (SAVED, GRAD, ACTS):
        slots_of(arr, ag_start)

    kept_back = kept[0, 0, 1:2, :].astype(F32)
    lens_back = lens[0, 0, 1:2, :].astype(F32)
    kept_fwd = kept[0, 0, 0:1, :].astype(F32)
    lens_fwd = lens[0, 0, 0:1, :].astype(F32)

    for load in loads:
        load.wait()

    for arr in (SAVED, GRAD):
        slots_of(arr, ag_pass)
    for arr in (SAVED, GRAD):

        def relay(arr, slot):
            dp_copy(arr, slot).wait_recv()
            ag_start(arr + 3, slot)

        slots_of(arr, relay)
    slots_of(ACTS, ag_pass)

    def rows_of(arr, slot):
        return buf[arr, slot].reshape(HALF_ROWS, width)

    def normalise(which, slab_of, slabs):
        def step(i, carry):
            x = slab_of(i).astype(F32)
            normed[which, pl.ds(pl.multiple_of(i * ROWS_PAD, ROWS_PAD), ROWS_PAD), :] = (
                x * inverse_root(x)
            ).astype(BF16)
            return carry

        lax.fori_loop(0, slabs, step, 0)

    def pick(arr, pos_col, into):
        chosen = select(pos_col, real_rows, keep)
        for n0 in range(0, width, 512):
            cols = slice(n0, n0 + 512)
            got = nn(chosen[:, :HALF_ROWS], buf[arr, 0, :, :, cols].reshape(HALF_ROWS, 512))
            got = got + nn(chosen[:, HALF_ROWS:], buf[arr, 1, :, :, cols].reshape(HALF_ROWS, 512))
            into[:, cols] = got.astype(BF16)

    def prepare(arr, which, kept_list):
        @pl.when(inner)
        def _():
            normalise(which, lambda i: buf[arr, 0, i], SLABS)

        @pl.when(first)
        def _():
            pick(arr, kept_positions(kept_list, real_rows), picked.at[which])
            normalise(
                which,
                lambda i: picked[which, pl.ds(pl.multiple_of(i * ROWS_PAD, ROWS_PAD), ROWS_PAD), :],
                SLABS,
            )

        @pl.when(last)
        def _():
            normalise(which, lambda i: buf[arr, i // SLABS, i % SLABS], 2 * SLABS)

    def places(kept_list, lengths, rows):
        pos_col = kept_positions(kept_list, real_rows)
        pos_row = to_row(pos_col)
        if rows > HALF_ROWS:
            more = dropped_positions(kept_list, real_rows)
            pos_row = jnp.concatenate([pos_row, more], axis=1)
            pos_col = jnp.concatenate([pos_col, to_col(more)], axis=0)
        allowed = (document_of(pos_col, lengths) == document_of(pos_row, lengths)) & (
            pos_row <= pos_col
        )
        return pos_col, allowed

    def heads(which, rows, allowed):
        x = normed[which, 0:rows, :]
        queries = nn(x, wq[...]).astype(BF16)
        keyval = nn(x, wkv[...]).astype(BF16)
        keys, values = keyval[:, :HEAD], keyval[:, HEAD:]
        out = []
        for h in range(2):
            q = queries[:, h * HEAD : (h + 1) * HEAD]
            scores = jnp.where(allowed, nt(q, keys) * HEAD ** (-0.5), -jnp.inf)
            e = jnp.exp(scores - jnp.max(scores, axis=1, keepdims=True))
            probs = e / jnp.sum(e, axis=1, keepdims=True)
            rounded = probs.astype(BF16)
            out.append((q, probs, rounded, nn(rounded, values).astype(BF16)))
        return keys, values, out

    def run_forward(rows):
        _, allowed = places(kept_fwd, lens_fwd, rows)
        _, _, out = heads(2, rows, allowed)
        mixed = jnp.concatenate([o[3] for o in out], axis=1)
        for n0 in range(0, width, 512):
            store_part(FORWARD, rows, n0, nn(mixed, wo[:, n0 : n0 + 512]))

    def store_part(f, rows, n0, value):
        value = value.astype(BF16)
        for slot in range(rows // HALF_ROWS):
            part[f, slot, :, :, n0 : n0 + 512] = value[
                slot * HALF_ROWS : (slot + 1) * HALF_ROWS
            ].reshape(SLABS, ROWS_PAD, 512)

    def cotangent(which, rows, pos_col):
        arr = GRAD + 3 * which
        if rows > HALF_ROWS:
            pick(arr, pos_col, gpick.at[which])
            return gpick[which]
        return rows_of(arr, 0)

    def run_back(which, rows, kept_list, lengths):
        pos_col, allowed = places(kept_list, lengths, rows)
        upstream = cotangent(which, rows, pos_col)
        grad_mixed = nt(upstream, wo[...]).astype(BF16)
        keys, values, out = heads(which, rows, allowed)
        grad_k = jnp.zeros((rows, HEAD), F32)
        grad_v = jnp.zeros((rows, HEAD), F32)
        grad_q = []
        for h, (q, probs, rounded, _) in enumerate(out):
            gm = grad_mixed[:, h * HEAD : (h + 1) * HEAD]
            grad_probs = nt(gm, values)
            centre = jnp.sum(probs * grad_probs, axis=1, keepdims=True)
            scores = (probs * (grad_probs - centre) * HEAD ** (-0.5)).astype(BF16)
            grad_q.append(nn(scores, keys).astype(BF16))
            grad_k = grad_k + tn(scores, q)
            grad_v = grad_v + tn(rounded, gm)
        gq = jnp.concatenate(grad_q, axis=1)
        gkv = jnp.concatenate([grad_k.astype(BF16), grad_v.astype(BF16)], axis=1)
        stash[which, 0, 0:rows, :] = gq
        stash[which, 1, 0:rows, :] = gkv
        stash[which, 2, 0:rows, :] = jnp.concatenate([o[3] for o in out], axis=1)
        if which == 0:
            for n0 in range(0, width, 512):
                term = nt(gq, wq[n0 : n0 + 512, :]) + nt(gkv, wkv[n0 : n0 + 512, :])
                store_part(BACK, rows, n0, term)

    def by_rows(run):
        @pl.when(jnp.logical_not(last))
        def _():
            run(HALF_ROWS)

        @pl.when(last)
        def _():
            run(2 * HALF_ROWS)

    def slots_rs(f, action):
        action(f, 0)

        @pl.when(last)
        def _():
            action(f, 1)

    def rs1(f, slot):
        return remote(
            part.at[f, slot, pl.ds((1 - c) * 4, 4)], sibrecv.at[f, slot],
            r1s.at[f, slot], r1r.at[f, slot], sibling,
        )

    def rs2(f, slot, d):
        return remote(
            chip.at[f, slot, peer_y(d)], yrecv.at[f, slot, y],
            r2s.at[f, slot, d - 1], r2r.at[f, slot, y], {"tensor": peer_y(d) * 2 + c},
        )

    def rs_cross(f, slot):
        rs1(f, slot).wait_recv()
        for d in (2, 1, 3):
            there = peer_y(d)
            total = part[f, slot, c * 4 + there].astype(F32) + sibrecv[f, slot, there].astype(F32)
            chip[f, slot, there] = total.astype(BF16)
            rs2(f, slot, d).start()

    def rs_total(f, slot):
        total = part[f, slot, own].astype(F32) + sibrecv[f, slot, y].astype(F32)
        for d in (1, 3, 2):
            there = peer_y(d)
            here = yrecv.at[f, slot, there]
            remote(here, here, r2s.at[f, slot, d - 1], r2r.at[f, slot, there], sibling).wait_recv()
            total = total + yrecv[f, slot, there].astype(F32)
        return total

    def rs_end(f, slot):
        rs1(f, slot).wait_send()
        for d in (1, 2, 3):
            rs2(f, slot, d).wait_send()

    def hand(f, slot, device):
        return remote(hsrc.at[f, slot], hrecv.at[f, slot], hs.at[f, slot], hr.at[f, slot], device)

    own_rows = pl.ds(pl.multiple_of(own * ROWS_PAD, ROWS_PAD), ROWS_PAD)

    for arr in (SAVED, GRAD):
        slots_of(arr, ag_wait)
    prepare(SAVED, 0, kept_back)
    by_rows(lambda rows: run_back(0, rows, kept_back, lens_back))
    slots_rs(BACK, lambda f, slot: rs1(f, slot).start())

    slots_of(ACTS, ag_wait)
    prepare(ACTS, 2, kept_fwd)
    slots_rs(BACK, rs_cross)
    by_rows(run_forward)
    slots_rs(FORWARD, lambda f, slot: rs1(f, slot).start())

    for arr in (SAVED_2, GRAD_2):
        slots_of(arr, ag_pass)
    slots_rs(FORWARD, rs_cross)

    @pl.when(first)
    def _():
        drop_row = dropped_positions(kept_fwd, real_rows)
        mine = iota((ROWS_PAD, HALF_ROWS), 1) == own * ROWS_PAD + iota((ROWS_PAD, HALF_ROWS), 0)
        drop_col = jnp.sum(jnp.where(mine, drop_row, 0.0), axis=1, keepdims=True)
        pick(ACTS, drop_col, hsrc.at[FORWARD, 1])
        hand(FORWARD, 1, prev_pipe).start()

    def finish_back(f, slot):
        total = rs_total(f, slot)

        def write(x, g):
            x, g = x.astype(F32), g.astype(F32)
            scale = inverse_root(x)
            unrounded = x * scale
            inner_mean = jnp.mean(total * unrounded, axis=1, keepdims=True)
            hsrc[f, slot] = (g + scale * (total - unrounded * inner_mean)).astype(BF16)

        @pl.when(inner)
        def _():
            write(buf[SAVED, slot, own], buf[GRAD, slot, own])

        @pl.when(first)
        def _():
            write(picked[0, own_rows, :], buf[GRAD, slot, own])

        @pl.when(last)
        def _():
            write(
                buf[SAVED, slot, own],
                gpick[0, pl.ds(pl.multiple_of(slot * HALF_ROWS + own * ROWS_PAD, ROWS_PAD), ROWS_PAD), :],
            )

        if slot == 0:

            @pl.when(jnp.logical_not(first))
            def _():
                hand(f, 0, prev_pipe).start()
        else:
            hand(f, 1, next_pipe).start()

    def finish_forward(f, slot):
        total = rs_total(f, slot)

        @pl.when(jnp.logical_not(first))
        def _():
            chip[f, slot, y] = (buf[ACTS, slot, own].astype(F32) + total).astype(BF16)

        @pl.when(first)
        def _():
            chip[f, slot, y] = (picked[2, own_rows, :].astype(F32) + total).astype(BF16)

        if slot == 0:
            hsrc[f, 0] = chip[f, 0, y]

            @pl.when(jnp.logical_not(last))
            def _():
                hand(f, 0, next_pipe).start()

    slots_rs(BACK, finish_back)
    slots_rs(FORWARD, finish_forward)

    for arr in (SAVED_2, GRAD_2):
        slots_of(arr, ag_wait)
    kept_copy.wait_recv()
    lens_copy.wait_recv()
    kept_two = kept2[1:2, :].astype(F32)
    lens_two = lens2[1:2, :].astype(F32)
    prepare(SAVED_2, 1, kept_two)
    by_rows(lambda rows: run_back(1, rows, kept_two, lens_two))

    columns = pl.ds(pl.multiple_of(r * half_width, half_width), half_width)

    def weights(rows):
        def stashed(which, i):
            return stash[which, i, 0:rows, :]

        def ups(which):
            if rows > HALF_ROWS:
                return gpick[which, :, columns]
            return buf[GRAD + 3 * which, 0, :, :, columns].reshape(HALF_ROWS, half_width)

        x0, x1 = normed[0, 0:rows, columns], normed[1, 0:rows, columns]
        gq_out[0] = (tn(x0, stashed(0, 0)) + tn(x1, stashed(1, 0))).astype(BF16)
        gkv_out[...] = (tn(x0, stashed(0, 1)) + tn(x1, stashed(1, 1))).astype(BF16)
        go_out[0] = (tn(stashed(0, 2), ups(0)) + tn(stashed(1, 2), ups(1))).astype(BF16)

    by_rows(weights)

    nothing = jnp.zeros((real_rows, width), BF16)

    def arrived(f, slot):
        hand(f, slot, next_pipe).wait_recv()
        return hrecv[f, slot, 0:real_rows, :]

    for f, out, none, both in ((FORWARD, handed, first, last), (BACK, back, last, first)):

        @pl.when(none)
        def _(out=out):
            out[0, 0, 0] = nothing

        @pl.when(jnp.logical_not(none))
        def _(f=f, out=out):
            out[0, 0, 0] = arrived(f, 0)

        @pl.when(jnp.logical_not(both))
        def _(out=out):
            out[0, 0, 1] = nothing

        @pl.when(both)
        def _(f=f, out=out):
            out[0, 0, 1] = arrived(f, 1)

    for arr in range(5):
        slots_of(arr, ag_end)
    for arr in (SAVED, GRAD):
        slots_of(arr, lambda arr, slot: dp_copy(arr, slot).wait_send())
    kept_copy.wait_send()
    lens_copy.wait_send()
    for f in (BACK, FORWARD):
        slots_rs(f, rs_end)

    @pl.when(jnp.logical_not(last))
    def _():
        hand(FORWARD, 0, next_pipe).wait_send()

    @pl.when(jnp.logical_not(first))
    def _():
        hand(BACK, 0, next_pipe).wait_send()

    @pl.when(first)
    def _():
        hand(FORWARD, 1, next_pipe).wait_send()

    @pl.when(last)
    def _():
        hand(BACK, 1, next_pipe).wait_send()


def local(acts_in, saved_in, out_grad, w_query, w_keyval, w_out, kept_rows, doc_lengths):
    width = acts_in.shape[4]
    cols = w_query.shape[2]
    slab = (ROWS_PAD, width)
    dma = pltpu.SemaphoreType.DMA
    vmem = pl.BlockSpec(memory_space=pltpu.VMEM)
    anywhere = pl.BlockSpec(memory_space=pl.ANY)
    handed, back, gq, gkv, go = pl.pallas_call(
        kernel,
        out_shape=(
            jax.ShapeDtypeStruct(acts_in.shape, BF16),
            jax.ShapeDtypeStruct(acts_in.shape, BF16),
            jax.ShapeDtypeStruct((1, width // 2, cols), BF16),
            jax.ShapeDtypeStruct((width // 2, 2 * HEAD), BF16),
            jax.ShapeDtypeStruct((1, cols, width // 2), BF16),
        ),
        in_specs=[vmem] * 5 + [anywhere] * 3,
        out_specs=[vmem] * 5,
        scratch_shapes=[
            pltpu.VMEM((5, 2, SLABS) + slab, BF16),
            pltpu.VMEM((width, cols), BF16),
            pltpu.VMEM((width, 2 * HEAD), BF16),
            pltpu.VMEM((cols, width), BF16),
            pltpu.VMEM(kept_rows.shape[2:], jnp.int32),
            pltpu.VMEM(doc_lengths.shape[2:], jnp.int32),
            pltpu.VMEM((3, 2 * HALF_ROWS, width), BF16),
            pltpu.VMEM((3, HALF_ROWS, width), BF16),
            pltpu.VMEM((2, 2 * HALF_ROWS, width), BF16),
            pltpu.VMEM((2, 3, 2 * HALF_ROWS, 2 * HEAD), BF16),
            pltpu.VMEM((2, 2, SLABS) + slab, BF16),
            pltpu.VMEM((2, 2, 4) + slab, BF16),
            pltpu.VMEM((2, 2, 4) + slab, BF16),
            pltpu.VMEM((2, 2, 4) + slab, BF16),
            pltpu.VMEM((2, 2) + slab, BF16),
            pltpu.VMEM((2, 2) + slab, BF16),
            dma((3,)),
            dma((3, 2)),
            dma((3, 2)),
            dma((5, 2, 7)),
            dma((5, 2, SLABS)),
            dma((2, 2)),
            dma((2, 2)),
            dma((2, 2, 3)),
            dma((2, 2, 4)),
            dma((2, 2)),
            dma((2, 2)),
        ],
        compiler_params=pltpu.CompilerParams(
            collective_id=0, has_side_effects=True, vmem_limit_bytes=56 * 1024 * 1024
        ),
        cost_estimate=pl.CostEstimate(flops=4_000_000_000, bytes_accessed=8_000_000, transcendentals=200_000),
        name="section",
    )(
        acts_in, saved_in, out_grad, kept_rows, doc_lengths, w_query,
        w_keyval.reshape(width, 2 * HEAD), w_out,
    )
    return (handed, back, gq, gkv.reshape(1, width // 2, 2, HEAD), go)


def solution(mesh):
    placed = (
        P("pipe", "dp", None, "tensor", None),
        P("pipe", "dp", None, "tensor", None),
        P("pipe", "dp", None, "tensor", None),
        P("pipe", None, "tensor"),
        P("pipe", None, None, "tensor"),
        P("pipe", "tensor", None),
        P("pipe", "dp", None, None),
        P("pipe", "dp", None, None),
    )
    return jax.shard_map(
        local,
        mesh=mesh,
        in_specs=placed,
        out_specs=(
            P("pipe", "dp", None, "tensor", None),
            P("pipe", "dp", None, "tensor", None),
            P("pipe", "dp", "tensor"),
            P("pipe", "dp", None, "tensor"),
            P("pipe", "tensor", "dp"),
        ),
        check_vma=False,
    )
```

```python
import jax
import jax.numpy as jnp
from jax import lax
from jax.experimental import pallas as pl
from jax.experimental.pallas import tpu as pltpu
from jax.sharding import PartitionSpec as P

HEAD = 128
EPSILON = 1e-06
MESH = pl.DeviceIdType.MESH
F32 = jnp.float32
BF16 = jnp.bfloat16

SAVED, GRAD, ACTS, SAVED_2, GRAD_2 = range(5)
BACK, FORWARD = 0, 1
ROWS_PAD = 16
SLABS = 8
HALF_ROWS = SLABS * ROWS_PAD


def nn(a, b):
    return lax.dot_general(a, b, (((1,), (0,)), ((), ())), preferred_element_type=F32)


def nt(a, b):
    return lax.dot_general(a, b, (((1,), (1,)), ((), ())), preferred_element_type=F32)


def tn(a, b):
    return lax.dot_general(a, b, (((0,), (0,)), ((), ())), preferred_element_type=F32)


def iota(shape, dim):
    return lax.broadcasted_iota(jnp.int32, shape, dim)


def list_index(a, real_rows):
    core, y, r = a // 64, (a // 16) % 4, a % 16
    return (2 * y + core) * real_rows + r, r < real_rows


def to_row(col):
    n = col.shape[0]
    return jnp.sum(jnp.where(iota((n, n), 0) == iota((n, n), 1), col, 0.0), axis=0, keepdims=True)


def to_col(row):
    n = row.shape[1]
    return jnp.sum(jnp.where(iota((n, n), 0) == iota((n, n), 1), row, 0.0), axis=1, keepdims=True)


def kept_positions(kept, real_rows):
    keep = kept.shape[1]
    place, real = list_index(iota((HALF_ROWS, keep), 0), real_rows)
    hit = (place == iota((HALF_ROWS, keep), 1)) & real
    found = jnp.sum(jnp.where(hit, kept, 0.0), axis=1, keepdims=True)
    _, real_col = list_index(iota((HALF_ROWS, 1), 0), real_rows)
    return jnp.where(real_col, found, 1000.0)


def dropped_positions(kept, real_rows):
    keep = kept.shape[1]
    n = 256
    named = jnp.max(
        jnp.where(iota((n, keep), 0).astype(F32) == kept, 1.0, 0.0), axis=1, keepdims=True
    )
    free = jnp.where(iota((n, 1), 0) < 2 * keep, 1.0 - named, 0.0)
    count = jnp.sum(
        jnp.where(iota((n, n), 1) <= iota((n, n), 0), to_row(free), 0.0), axis=1, keepdims=True
    )
    place, real = list_index(iota((n, HALF_ROWS), 1), real_rows)
    hit = (count - 1.0 == place.astype(F32)) & (free > 0.5) & real
    found = jnp.sum(jnp.where(hit, iota((n, HALF_ROWS), 0).astype(F32), 0.0), axis=0, keepdims=True)
    _, real_row = list_index(iota((1, HALF_ROWS), 1), real_rows)
    return jnp.where(real_row, found, 1000.0)


def document_of(positions, lengths):
    bound = jnp.zeros((1, 1), F32)
    total = jnp.zeros(positions.shape, F32)
    for m in range(lengths.shape[1]):
        bound = bound + lengths[:, m : m + 1]
        total = total + jnp.where(positions >= bound, 1.0, 0.0)
    return total


def select(pos_col, real_rows, keep):
    n = 2 * HALF_ROWS
    b = iota((1, n), 1)
    place, real = list_index(b % HALF_ROWS, real_rows)
    flat = jnp.where(real, (b // HALF_ROWS) * keep + place, -1).astype(F32)
    return jnp.where(pos_col == flat, 1.0, 0.0).astype(BF16)


def line_of(q, width):
    tile, slot, r = q // (2 * ROWS_PAD), (q // ROWS_PAD) % 2, q % ROWS_PAD
    quarter = width // HEAD // 4
    spill = r >= 12
    row = jnp.where(spill, 4 * (tile // quarter) + r - 12, r)
    place = jnp.where(spill, 3 * quarter + tile % quarter, tile)
    return (row * (4 * quarter) + place) * 2 + slot


def unpack(x):
    w = x.shape[1] // 3
    r = iota((ROWS_PAD, 1), 0)
    tail = jnp.where(
        r < 4,
        pltpu.roll(x[:, :w], 4, 0),
        jnp.where(r < 8, pltpu.roll(x[:, w : 2 * w], 8, 0), pltpu.roll(x[:, 2 * w :], 12, 0)),
    )
    return jnp.where(r < 12, jnp.concatenate([x, tail], axis=1), 0.0)


def pack(parts, tail):
    r = iota((tail.shape[0], 1), 0) % ROWS_PAD
    return [jnp.where(r < 12, x, pltpu.roll(tail, 12 - 4 * i, 0)) for i, x in enumerate(parts)]


def pack_slab(x):
    w = x.shape[1] // 4
    return jnp.concatenate(pack([x[:, i * w : (i + 1) * w] for i in range(3)], x[:, 3 * w :]), axis=1)


def pairs_apart():
    n = 2 * HEAD
    q, k = iota((n, n), 0), iota((n, n), 1)
    return jnp.where((q % HEAD) * 2 + q // HEAD == k, 1.0, 0.0).astype(BF16)


def inverse_root(x):
    return lax.rsqrt(jnp.mean(x * x, axis=1, keepdims=True) + EPSILON)


def kernel(
    acts_hbm, saved_hbm, ograd_hbm, kept_hbm, lens_hbm, wq_hbm, wkv_hbm, wo_hbm,
    handed_out, back_out, gq_out, gkv_out, go_out,
    acts, saved, ograd, kept, lens, buf, wq, wkv, wkv_pairs, wo, kept2, lens2, normed, raw, picked, chosen, stash, part, sibrecv, chip, yrecv, hsrc, hrecv,
    tiles, handed, back, gq, gkv, go,
    wsem, osem, dps, dpr, ags, agr, r1s, r1r, r2s, r2r, hs, hr,
):
    pipes = lax.axis_size("pipe")
    p, r, t = lax.axis_index("pipe"), lax.axis_index("dp"), lax.axis_index("tensor")
    y, c = t // 2, t % 2
    own = c * 4 + y
    first, last = p == 0, p == pipes - 1
    inner = jnp.logical_not(first | last)
    width = wq.shape[0]
    real_rows = acts.shape[0] * HEAD // (2 * width)
    keep = kept.shape[3]
    half_width, packed, quarter = width // 2, 3 * width // 4, width // 4
    next_pipe = {"pipe": lax.rem(p + 1, pipes)}
    prev_pipe = {"pipe": lax.rem(p + pipes - 1, pipes)}
    sibling = {"tensor": y * 2 + 1 - c}
    other_dp = {"dp": 1 - r}

    def peer_y(d):
        return lax.rem(y + d, 4)

    def remote(src, dst, send, recv, device):
        return pltpu.make_async_remote_copy(
            src_ref=src, dst_ref=dst, send_sem=send, recv_sem=recv, device_id=device, device_id_type=MESH
        )

    barrier = pltpu.get_barrier_semaphore()
    greet = [{"tensor": lax.rem(t + d, 8)} for d in range(1, 8)] + [other_dp, next_pipe, prev_pipe]
    for device in greet:
        pl.semaphore_signal(barrier, inc=1, device_id=device, device_id_type=MESH)

    loads = [
        pltpu.make_async_copy(src, dst, wsem.at[i])
        for i, (src, dst) in enumerate(
            (
                (saved_hbm, saved),
                (ograd_hbm, ograd),
                (acts_hbm, acts),
                (kept_hbm, kept),
                (lens_hbm, lens),
                (wkv_hbm, wkv_pairs),
                (wq_hbm.at[0], wq),
                (wo_hbm.at[0], wo),
            )
        )
    ]
    for load in loads:
        load.start()
    stores = [
        pltpu.make_async_copy(src, dst, osem.at[i])
        for i, (src, dst) in enumerate(
            ((handed, handed_out), (back, back_out), (gq, gq_out), (gkv, gkv_out), (go, go_out))
        )
    ]
    tiles[...] = jnp.zeros_like(tiles)

    lines = acts.shape[0]
    q, k = iota((lines, lines), 0), iota((lines, lines), 1)
    spread = jnp.where(line_of(q, width) == k, 1.0, 0.0).astype(BF16)
    for load in loads[:5]:
        load.wait()
    rows = nn(spread, jnp.concatenate([saved[...], ograd[...], acts[...]], axis=1)).astype(BF16)
    for ct in range(packed // HEAD):
        for slot in range(2):
            for arr in (SAVED, GRAD, ACTS):
                at = (2 * ct + slot) * ROWS_PAD
                buf[arr, slot, own, :, ct * HEAD : (ct + 1) * HEAD] = rows[
                    at : at + ROWS_PAD, arr * HEAD : (arr + 1) * HEAD
                ]

    pl.semaphore_wait(barrier, len(greet))

    def dp_copy(arr, slot):
        return remote(
            buf.at[arr, slot, own], buf.at[arr + 3, slot, own],
            dps.at[arr, slot], dpr.at[arr, slot], other_dp,
        )

    kept_copy = remote(kept.at[0, 0], kept2, dps.at[2, 0], dpr.at[2, 0], other_dp)
    lens_copy = remote(lens.at[0, 0], lens2, dps.at[2, 1], dpr.at[2, 1], other_dp)

    def slab_to(arr, slot, slab, sem, device):
        here = buf.at[arr, slot, slab]
        return remote(here, here, ags.at[arr, slot, sem], agr.at[arr, slot, slab], device)

    def across(sem, slab, arr, slot, d):
        slab_to(arr, slot, slab, sem, {"tensor": peer_y(d) * 2 + c}).start()

    def ag_take(arr, slot, d):
        copy = slab_to(arr, slot, c * 4 + peer_y(d), 3 + d, sibling)
        copy.wait_recv()
        copy.start()

    def ag_rest(arr, slot):
        ag_take(arr, slot, 1 if (arr + slot) % 2 == 0 else 3)
        ag_take(arr, slot, 2)

    def ag_wait(arr, slot):
        for d in range(4):
            slab_to(arr, slot, (1 - c) * 4 + peer_y(d), 3, sibling).wait_recv()

    def ag_end(arr, slot):
        for d in range(7):
            slab_to(arr, slot, own, d, sibling).wait_send()

    def split_weights():
        loads[5].wait()
        apart = pairs_apart()

        def split(i, carry):
            two = pl.multiple_of(i * 512, 512)
            pairs = jnp.concatenate(
                [wkv_pairs[pl.ds(two, 256), :], wkv_pairs[pl.ds(two + 256, 256), :]], axis=1
            )
            got = nn(apart, pairs).astype(BF16)
            for j in range(2):
                at = pl.ds(pl.multiple_of(i * 256 + j * 128, 128), 128)
                cols = slice(j * HEAD, (j + 1) * HEAD)
                wkv[at, 0:HEAD] = got[:HEAD, cols]
                wkv[at, HEAD:] = got[HEAD:, cols]
            return carry

        lax.fori_loop(0, width // 256, split, 0)
        for load in loads[6:]:
            load.wait()

    def slab_rows(i):
        return pl.ds(pl.multiple_of(i * ROWS_PAD, ROWS_PAD), ROWS_PAD)

    def for_slabs(slabs, step):
        lax.fori_loop(0, slabs, lambda i, carry: step(i) or carry, 0, unroll=2)

    def received(arr, i):
        return unpack(buf[arr, i // SLABS, i % SLABS].astype(F32))

    def to_raw(arr, slabs):
        def step(i):
            raw[arr, slab_rows(i), :] = received(arr, i).astype(BF16)

        for_slabs(slabs, step)

    def normalise(which, slab_of, slabs):
        def step(i):
            x = slab_of(i)
            normed[which, slab_rows(i), :] = (x * inverse_root(x)).astype(BF16)

        for_slabs(slabs, step)

    def places(kept_list, lengths, rows):
        pos_col = kept_positions(kept_list, real_rows)
        pos_row = to_row(pos_col)
        if rows > HALF_ROWS:
            more = dropped_positions(kept_list, real_rows)
            pos_row = jnp.concatenate([pos_row, more], axis=1)
            pos_col = jnp.concatenate([pos_col, to_col(more)], axis=0)
        allowed = (document_of(pos_col, lengths) == document_of(pos_row, lengths)) & (
            pos_row <= pos_col
        )
        return pos_col, allowed

    def heads(which, rows, allowed):
        x = normed[which, 0:rows, :]
        queries = nn(x, wq[...]).astype(BF16)
        keyval = nn(x, wkv[...]).astype(BF16)
        keys, values = keyval[:, :HEAD], keyval[:, HEAD:]
        out = []
        for h in range(2):
            q = queries[:, h * HEAD : (h + 1) * HEAD]
            scores = jnp.where(allowed, nt(q, keys) * HEAD ** (-0.5), -jnp.inf)
            e = jnp.exp(scores - jnp.max(scores, axis=1, keepdims=True))
            probs = e / jnp.sum(e, axis=1, keepdims=True)
            rounded = probs.astype(BF16)
            out.append((q, probs, rounded, nn(rounded, values).astype(BF16)))
        return keys, values, out

    def store_part(f, rows, term):
        packs = pack([term(i * quarter) for i in range(3)], term(3 * quarter))
        for i, value in enumerate(packs):
            value = value.astype(BF16)
            for slot in range(rows // HALF_ROWS):
                part[f, slot, :, :, i * quarter : (i + 1) * quarter] = value[
                    slot * HALF_ROWS : (slot + 1) * HALF_ROWS
                ].reshape(SLABS, ROWS_PAD, quarter)

    def run_forward(rows, allowed):
        _, _, out = heads(2, rows, allowed)
        mixed = jnp.concatenate([o[3] for o in out], axis=1)
        store_part(FORWARD, rows, lambda n0: nn(mixed, wo[:, n0 : n0 + quarter]))

    def run_back(which, rows, pos_col, allowed, middle, late):
        keys, values, out = heads(which, rows, allowed)
        middle()
        to_raw(GRAD + 3 * which, rows // ROWS_PAD)
        upstream = raw[GRAD + 3 * which, 0:rows, :]
        grad_mixed = nt(upstream, wo[...]).astype(BF16)
        mixed = jnp.concatenate([o[3] for o in out], axis=1)
        if rows > HALF_ROWS:
            picks = select(pos_col, real_rows, keep)
            grad_mixed = nn(picks, grad_mixed).astype(BF16)
            mixed = tn(picks, mixed).astype(BF16)
            if which == 0:
                chosen[...] = picks
        grad_k = jnp.zeros((rows, HEAD), F32)
        grad_v = jnp.zeros((rows, HEAD), F32)
        grad_q = []
        for h, (q, probs, rounded, _) in enumerate(out):
            gm = grad_mixed[:, h * HEAD : (h + 1) * HEAD]
            grad_probs = nt(gm, values)
            centre = jnp.sum(probs * grad_probs, axis=1, keepdims=True)
            scores = (probs * (grad_probs - centre) * HEAD ** (-0.5)).astype(BF16)
            grad_q.append(nn(scores, keys).astype(BF16))
            grad_k = grad_k + tn(scores, q)
            grad_v = grad_v + tn(rounded, gm)
        gq_rows = jnp.concatenate(grad_q, axis=1)
        gkv_rows = jnp.concatenate([grad_k.astype(BF16), grad_v.astype(BF16)], axis=1)
        stash[which, 0, 0:rows, :] = gq_rows
        stash[which, 1, 0:rows, :] = gkv_rows
        stash[which, 2, 0:rows, :] = mixed
        late()
        if which == 0:
            store_part(
                BACK,
                rows,
                lambda n0: nt(gq_rows, wq[n0 : n0 + quarter, :]) + nt(gkv_rows, wkv[n0 : n0 + quarter, :]),
            )

    def rs1(f, slot):
        return remote(
            part.at[f, slot, pl.ds((1 - c) * 4, 4)], sibrecv.at[f, slot],
            r1s.at[f, slot], r1r.at[f, slot], sibling,
        )

    def rs_send(f, slot):
        rs1(f, slot).start()

    def rs2(f, slot, d):
        return remote(
            chip.at[f, slot, peer_y(d)], yrecv.at[f, slot, y],
            r2s.at[f, slot, d - 1], r2r.at[f, slot, y], {"tensor": peer_y(d) * 2 + c},
        )

    def rs_cross(f, slot):
        rs1(f, slot).wait_recv()
        for d in (2, 1, 3):
            there = peer_y(d)
            total = part[f, slot, c * 4 + there].astype(F32) + sibrecv[f, slot, there].astype(F32)
            chip[f, slot, there] = total.astype(BF16)
            rs2(f, slot, d).start()

    def rs_total(f, slot):
        total = part[f, slot, own].astype(F32) + sibrecv[f, slot, y].astype(F32)
        for d in (1, 3, 2):
            there = peer_y(d)
            here = yrecv.at[f, slot, there]
            remote(here, here, r2s.at[f, slot, d - 1], r2r.at[f, slot, there], sibling).wait_recv()
            total = total + yrecv[f, slot, there].astype(F32)
        return unpack(total)

    def rs_end(f, slot):
        rs1(f, slot).wait_send()
        for d in (1, 2, 3):
            rs2(f, slot, d).wait_send()

    def hand(f, slot, device):
        return remote(hsrc.at[f, slot], hrecv.at[f, slot], hs.at[f, slot], hr.at[f, slot], device)

    columns = pl.ds(pl.multiple_of(r * half_width, half_width), half_width)

    def weights(rows):
        def stashed(which, i):
            return stash[which, i, 0:rows, :]

        def ups(which):
            return raw[GRAD + 3 * which, 0:rows, columns]

        x0, x1 = normed[0, 0:rows, columns], normed[1, 0:rows, columns]
        go[...] = (tn(stashed(0, 2), ups(0)) + tn(stashed(1, 2), ups(1))).astype(BF16)
        stores[4].start()
        gq[...] = (tn(x0, stashed(0, 0)) + tn(x1, stashed(1, 0))).astype(BF16)
        stores[2].start()
        both = (tn(x0, stashed(0, 1)) + tn(x1, stashed(1, 1))).astype(BF16)
        joined = jnp.transpose(pairs_apart().astype(F32)).astype(BF16)
        for i in range(half_width // HEAD):
            block = both[i * HEAD : (i + 1) * HEAD]
            block = jnp.concatenate([block[:, :HEAD], block[:, HEAD:]], axis=0)
            gkv[i * 256 : (i + 1) * 256, :] = nn(joined, block).astype(BF16)
        stores[3].start()

    def section(at_first, at_last):
        rows = 2 * HALF_ROWS if at_last else HALF_ROWS
        ends = at_first or at_last

        def slots_of(arr, action):
            two = at_last or (at_first and arr not in (GRAD, GRAD_2))
            for slot in range(2 if two else 1):
                action(arr, slot)

        def slots_rs(f, action):
            for slot in (1, 0) if at_last else (0,):
                action(f, slot)

        def ag_start(arr, slot):
            if not ends:
                across(1, own, arr, slot, 2)
            across(0, own, arr, slot, 1)
            across(2, own, arr, slot, 3)
            slab_to(arr, slot, own, 3, sibling).start()

        def ag_near(arr, slot):
            source, target = (3, 1) if (arr + slot) % 2 == 0 else (1, 3)
            ag_take(arr, slot, source)
            if ends:
                across(1, c * 4 + peer_y(source), arr, slot, target)

        def near(*arrs):
            for arr in arrs:
                slots_of(arr, ag_near)

        def rest(*arrs):
            for arr in arrs:
                slots_of(arr, ag_rest)

        def relay():
            def one(arr, slot):
                dp_copy(arr, slot).wait_recv()
                ag_start(arr + 3, slot)

            slots_of(SAVED, one)
            slots_of(GRAD, one)

        def prepare(arr, which, pos_col):
            slots_of(arr, ag_wait)
            if at_first:
                to_raw(arr, 2 * SLABS)
                picks = select(pos_col, real_rows, keep)
                for n0 in range(0, width, quarter):
                    picked[which, :, n0 : n0 + quarter] = nn(
                        picks, raw[arr, :, n0 : n0 + quarter]
                    ).astype(BF16)
                normalise(which, lambda i: picked[which, slab_rows(i), :].astype(F32), SLABS)
            else:
                normalise(which, lambda i: received(arr, i), rows // ROWS_PAD)

        def finish_back(f, slot):
            total = rs_total(f, slot)
            at = slot * SLABS + own
            x = picked[0, slab_rows(own), :].astype(F32) if at_first else received(SAVED, at)
            if at_last:
                g = nn(chosen[slab_rows(at), :], raw[GRAD])
            else:
                g = raw[GRAD, slab_rows(own), :].astype(F32)
            scale = inverse_root(x)
            unrounded = x * scale
            inner_mean = jnp.mean(total * unrounded, axis=1, keepdims=True)
            hsrc[f, slot] = pack_slab(g + scale * (total - unrounded * inner_mean)).astype(BF16)
            if slot == 1:
                hand(f, 1, next_pipe).start()
            elif not at_first:
                hand(f, 0, prev_pipe).start()

        def finish_forward(f, slot):
            total = rs_total(f, slot)
            x = picked[2, slab_rows(own), :].astype(F32) if at_first else received(ACTS, slot * SLABS + own)
            hsrc[f, slot] = pack_slab(x + total).astype(BF16)
            if not at_last:
                hand(f, 0, next_pipe).start()

        def nothing():
            pass

        slots_of(SAVED, lambda arr, slot: dp_copy(arr, slot).start())
        slots_of(GRAD, lambda arr, slot: dp_copy(arr, slot).start())
        kept_copy.start()
        lens_copy.start()
        for arr in (SAVED, GRAD) if at_last else (ACTS, SAVED, GRAD):
            slots_of(arr, ag_start)
        split_weights()
        pos_fwd, allowed_fwd = places(kept[0, 0, 0:1, :].astype(F32), lens[0, 0, 0:1, :].astype(F32), rows)
        pos_back, allowed_back = places(kept[0, 0, 1:2, :].astype(F32), lens[0, 0, 1:2, :].astype(F32), rows)

        if at_last:
            near(SAVED, GRAD)
            slots_of(ACTS, ag_start)
            rest(SAVED, GRAD)
            prepare(SAVED, 0, pos_back)

            def middle():
                near(ACTS)
                slots_of(GRAD, ag_wait)

            run_back(0, rows, pos_back, allowed_back, middle, lambda: rest(ACTS))
            slots_rs(BACK, rs_send)
            slots_rs(BACK, rs_cross)
            relay()
            prepare(ACTS, 2, pos_fwd)
            slots_rs(BACK, finish_back)
            near(SAVED_2, GRAD_2)
            run_forward(rows, allowed_fwd)
            slots_rs(FORWARD, rs_send)
            rest(SAVED_2, GRAD_2)
            slots_rs(FORWARD, rs_cross)
        else:
            near(ACTS)
            if at_first:
                near(SAVED, GRAD)
            rest(ACTS)
            prepare(ACTS, 2, pos_fwd)
            if at_first:
                drop_row = dropped_positions(kept[0, 0, 0:1, :].astype(F32), real_rows)
                mine = iota((ROWS_PAD, HALF_ROWS), 1) == own * ROWS_PAD + iota((ROWS_PAD, HALF_ROWS), 0)
                drop_col = jnp.sum(jnp.where(mine, drop_row, 0.0), axis=1, keepdims=True)
                hsrc[FORWARD, 1] = pack_slab(nn(select(drop_col, real_rows, keep), raw[ACTS])).astype(BF16)
                hand(FORWARD, 1, prev_pipe).start()
            run_forward(rows, allowed_fwd)
            slots_rs(FORWARD, rs_send)
            if not at_first:
                near(SAVED, GRAD)
            rest(SAVED, GRAD)
            slots_rs(FORWARD, rs_cross)
            prepare(SAVED, 0, pos_back)
            run_back(0, rows, pos_back, allowed_back, lambda: slots_of(GRAD, ag_wait), nothing)
            slots_rs(BACK, rs_send)
            slots_rs(FORWARD, finish_forward)
            slots_rs(BACK, rs_cross)
            relay()
            slots_rs(BACK, finish_back)
            near(SAVED_2, GRAD_2)
            rest(SAVED_2, GRAD_2)

        kept_copy.wait_recv()
        lens_copy.wait_recv()
        pos_two, allowed_two = places(kept2[1:2, :].astype(F32), lens2[1:2, :].astype(F32), rows)
        prepare(SAVED_2, 1, pos_two)
        run_back(1, rows, pos_two, allowed_two, lambda: slots_of(GRAD_2, ag_wait), nothing)
        if at_last:
            slots_rs(FORWARD, finish_forward)
        weights(rows)

        for f, none, two in ((FORWARD, at_first, at_last), (BACK, at_last, at_first)):
            for slot in ([] if none else [0]) + ([1] if two else []):
                hand(f, slot, next_pipe).wait_recv()
                for ct in range(packed // HEAD):
                    at = (2 * ct + slot) * ROWS_PAD
                    tiles[at : at + ROWS_PAD, f * HEAD : (f + 1) * HEAD] = hrecv[
                        f, slot, :, ct * HEAD : (ct + 1) * HEAD
                    ]
        q, k = iota((lines, lines), 1), iota((lines, lines), 0)
        gather = jnp.where(line_of(q, width) == k, 1.0, 0.0).astype(BF16)
        found = nn(gather, tiles[...]).astype(BF16)
        handed[...] = found[:, FORWARD * HEAD : (FORWARD + 1) * HEAD]
        back[...] = found[:, BACK * HEAD : (BACK + 1) * HEAD]
        stores[0].start()
        stores[1].start()

        for arr in range(5):
            slots_of(arr, ag_end)
        for arr in (SAVED, GRAD):
            slots_of(arr, lambda arr, slot: dp_copy(arr, slot).wait_send())
        kept_copy.wait_send()
        lens_copy.wait_send()
        for f in (BACK, FORWARD):
            slots_rs(f, rs_end)
        if not at_last:
            hand(FORWARD, 0, next_pipe).wait_send()
        if not at_first:
            hand(BACK, 0, next_pipe).wait_send()
        if at_first:
            hand(FORWARD, 1, next_pipe).wait_send()
        if at_last:
            hand(BACK, 1, next_pipe).wait_send()
        for store in stores:
            store.wait()

    pl.when(inner)(lambda: section(False, False))
    pl.when(first)(lambda: section(True, False))
    pl.when(last)(lambda: section(False, True))


def copy_kernel(*refs):
    ins, outs, held, load, store = refs[:5], refs[5:10], refs[10:15], refs[15], refs[16]
    loads = [pltpu.make_async_copy(ins[i], held[i], load.at[i]) for i in range(5)]
    stores = [pltpu.make_async_copy(held[i], outs[i], store.at[i]) for i in range(5)]
    for copy in loads:
        copy.start()
    for i in range(5):
        loads[i].wait()
        stores[i].start()
    for copy in stores:
        copy.wait()


def lines_of(x):
    _, _, slots, rows, width = x.shape
    x = x.reshape(slots, rows, width // HEAD, HEAD)
    return jnp.transpose(x, (1, 2, 0, 3)).reshape(-1, HEAD)


def from_lines(x, shape):
    _, _, slots, rows, width = shape
    x = x.reshape(rows, width // HEAD, slots, HEAD)
    return jnp.transpose(x, (2, 0, 1, 3)).reshape(shape)


def local(acts_in, saved_in, out_grad, w_query, w_keyval, w_out, kept_rows, doc_lengths):
    width = acts_in.shape[4]
    cols = w_query.shape[2]
    slab = (ROWS_PAD, 3 * width // 4)
    lines = 2 * acts_in.shape[3] * width // HEAD
    dma = pltpu.SemaphoreType.DMA
    anywhere = pl.BlockSpec(memory_space=pl.ANY)
    outs = ((lines, HEAD), (lines, HEAD), (width // 2, cols), (width, HEAD), (cols, width // 2))
    out_shape = tuple(jax.ShapeDtypeStruct(shape, BF16) for shape in outs)
    results = pl.pallas_call(
        kernel,
        out_shape=out_shape,
        in_specs=[anywhere] * 8,
        out_specs=[anywhere] * 5,
        scratch_shapes=[pltpu.VMEM((lines, HEAD), BF16)] * 3
        + [
            pltpu.VMEM(kept_rows.shape, jnp.int32),
            pltpu.VMEM(doc_lengths.shape, jnp.int32),
            pltpu.VMEM((5, 2, SLABS) + slab, BF16),
            pltpu.VMEM((width, cols), BF16),
            pltpu.VMEM((width, 2 * HEAD), BF16),
            pltpu.VMEM((2 * width, HEAD), BF16),
            pltpu.VMEM((cols, width), BF16),
            pltpu.VMEM(kept_rows.shape[2:], jnp.int32),
            pltpu.VMEM(doc_lengths.shape[2:], jnp.int32),
            pltpu.VMEM((3, 2 * HALF_ROWS, width), BF16),
            pltpu.VMEM((5, 2 * HALF_ROWS, width), BF16),
            pltpu.VMEM((3, HALF_ROWS, width), BF16),
            pltpu.VMEM((2 * HALF_ROWS, 2 * HALF_ROWS), BF16),
            pltpu.VMEM((2, 3, 2 * HALF_ROWS, 2 * HEAD), BF16),
            pltpu.VMEM((2, 2, SLABS) + slab, BF16),
            pltpu.VMEM((2, 2, 4) + slab, BF16),
            pltpu.VMEM((2, 2, 4) + slab, BF16),
            pltpu.VMEM((2, 2, 4) + slab, BF16),
            pltpu.VMEM((2, 2) + slab, BF16),
            pltpu.VMEM((2, 2) + slab, BF16),
            pltpu.VMEM((lines, 2 * HEAD), BF16),
        ]
        + [pltpu.VMEM(shape, BF16) for shape in outs]
        + [
            dma((8,)),
            dma((5,)),
            dma((3, 2)),
            dma((3, 2)),
            dma((5, 2, 7)),
            dma((5, 2, SLABS)),
            dma((2, 2)),
            dma((2, 2)),
            dma((2, 2, 3)),
            dma((2, 2, 4)),
            dma((2, 2)),
            dma((2, 2)),
        ],
        compiler_params=pltpu.CompilerParams(
            collective_id=0, has_side_effects=True, vmem_limit_bytes=56 * 1024 * 1024
        ),
        cost_estimate=pl.CostEstimate(flops=4_000_000_000, bytes_accessed=8_000_000, transcendentals=200_000),
        name="section",
    )(
        lines_of(acts_in), lines_of(saved_in), lines_of(out_grad), kept_rows, doc_lengths, w_query,
        w_keyval.reshape(2 * width, HEAD), w_out,
    )
    handed, back, gq, gkv, go = pl.pallas_call(
        copy_kernel,
        out_shape=out_shape,
        in_specs=[anywhere] * 5,
        out_specs=[anywhere] * 5,
        scratch_shapes=[pltpu.VMEM(shape, BF16) for shape in outs] + [dma((5,)), dma((5,))],
        cost_estimate=pl.CostEstimate(flops=0, bytes_accessed=4_000_000, transcendentals=0),
        name="results",
    )(*results)
    return (
        from_lines(handed, acts_in.shape),
        from_lines(back, acts_in.shape),
        gq[None],
        gkv.reshape(1, width // 2, 2, HEAD),
        go[None],
    )


def solution(mesh):
    placed = (
        P("pipe", "dp", None, "tensor", None),
        P("pipe", "dp", None, "tensor", None),
        P("pipe", "dp", None, "tensor", None),
        P("pipe", None, "tensor"),
        P("pipe", None, None, "tensor"),
        P("pipe", "tensor", None),
        P("pipe", "dp", None, None),
        P("pipe", "dp", None, None),
    )
    return jax.shard_map(
        local,
        mesh=mesh,
        in_specs=placed,
        out_specs=(
            P("pipe", "dp", None, "tensor", None),
            P("pipe", "dp", None, "tensor", None),
            P("pipe", "dp", "tensor"),
            P("pipe", "dp", None, "tensor"),
            P("pipe", "tensor", "dp"),
        ),
        check_vma=False,
    )
```

```python
import jax
import jax.numpy as jnp
from jax import lax
from jax.experimental import pallas as pl
from jax.experimental.pallas import tpu as pltpu
from jax.sharding import PartitionSpec as P

HEAD = 128
EPSILON = 1e-06
MESH = pl.DeviceIdType.MESH
F32 = jnp.float32
BF16 = jnp.bfloat16

SAVED, GRAD, ACTS, SAVED_2, GRAD_2 = range(5)
BACK, FORWARD = 0, 1
ROWS_PAD = 16
SLABS = 8
HALF_ROWS = SLABS * ROWS_PAD


def nn(a, b):
    return lax.dot_general(a, b, (((1,), (0,)), ((), ())), preferred_element_type=F32)


def nt(a, b):
    return lax.dot_general(a, b, (((1,), (1,)), ((), ())), preferred_element_type=F32)


def tn(a, b):
    return lax.dot_general(a, b, (((0,), (0,)), ((), ())), preferred_element_type=F32)


def iota(shape, dim):
    return lax.broadcasted_iota(jnp.int32, shape, dim)


def list_index(a, real_rows):
    core, y, r = a // 64, (a // 16) % 4, a % 16
    return (2 * y + core) * real_rows + r, r < real_rows


def to_row(col):
    n = col.shape[0]
    return jnp.sum(jnp.where(iota((n, n), 0) == iota((n, n), 1), col, 0.0), axis=0, keepdims=True)


def to_col(row):
    n = row.shape[1]
    return jnp.sum(jnp.where(iota((n, n), 0) == iota((n, n), 1), row, 0.0), axis=1, keepdims=True)


def kept_positions(kept, real_rows):
    keep = kept.shape[1]
    place, real = list_index(iota((HALF_ROWS, keep), 0), real_rows)
    hit = (place == iota((HALF_ROWS, keep), 1)) & real
    found = jnp.sum(jnp.where(hit, kept, 0.0), axis=1, keepdims=True)
    _, real_col = list_index(iota((HALF_ROWS, 1), 0), real_rows)
    return jnp.where(real_col, found, 1000.0)


def dropped_positions(kept, real_rows):
    keep = kept.shape[1]
    n = 256
    named = jnp.max(
        jnp.where(iota((n, keep), 0).astype(F32) == kept, 1.0, 0.0), axis=1, keepdims=True
    )
    free = jnp.where(iota((n, 1), 0) < 2 * keep, 1.0 - named, 0.0)
    count = jnp.sum(
        jnp.where(iota((n, n), 1) <= iota((n, n), 0), to_row(free), 0.0), axis=1, keepdims=True
    )
    place, real = list_index(iota((n, HALF_ROWS), 1), real_rows)
    hit = (count - 1.0 == place.astype(F32)) & (free > 0.5) & real
    found = jnp.sum(jnp.where(hit, iota((n, HALF_ROWS), 0).astype(F32), 0.0), axis=0, keepdims=True)
    _, real_row = list_index(iota((1, HALF_ROWS), 1), real_rows)
    return jnp.where(real_row, found, 1000.0)


def document_of(positions, lengths):
    bound = jnp.zeros((1, 1), F32)
    total = jnp.zeros(positions.shape, F32)
    for m in range(lengths.shape[1]):
        bound = bound + lengths[:, m : m + 1]
        total = total + jnp.where(positions >= bound, 1.0, 0.0)
    return total


def select(pos_col, real_rows, keep):
    n = 2 * HALF_ROWS
    b = iota((1, n), 1)
    place, real = list_index(b % HALF_ROWS, real_rows)
    flat = jnp.where(real, (b // HALF_ROWS) * keep + place, -1).astype(F32)
    return jnp.where(pos_col == flat, 1.0, 0.0).astype(BF16)


def line_of(q, width):
    tile, slot, r = q // (2 * ROWS_PAD), (q // ROWS_PAD) % 2, q % ROWS_PAD
    quarter = width // HEAD // 4
    spill = r >= 12
    row = jnp.where(spill, 4 * (tile // quarter) + r - 12, r)
    place = jnp.where(spill, 3 * quarter + tile % quarter, tile)
    return (row * (4 * quarter) + place) * 2 + slot


def unpack(x):
    w = x.shape[1] // 3
    r = iota((ROWS_PAD, 1), 0)
    tail = jnp.where(
        r < 4,
        pltpu.roll(x[:, :w], 4, 0),
        jnp.where(r < 8, pltpu.roll(x[:, w : 2 * w], 8, 0), pltpu.roll(x[:, 2 * w :], 12, 0)),
    )
    return jnp.where(r < 12, jnp.concatenate([x, tail], axis=1), 0.0)


def pack(parts, tail):
    r = iota((tail.shape[0], 1), 0) % ROWS_PAD
    return [jnp.where(r < 12, x, pltpu.roll(tail, 12 - 4 * i, 0)) for i, x in enumerate(parts)]


def pack_slab(x):
    w = x.shape[1] // 4
    return jnp.concatenate(pack([x[:, i * w : (i + 1) * w] for i in range(3)], x[:, 3 * w :]), axis=1)


def pairs_apart():
    n = 2 * HEAD
    q, k = iota((n, n), 0), iota((n, n), 1)
    return jnp.where((q % HEAD) * 2 + q // HEAD == k, 1.0, 0.0).astype(BF16)


def inverse_root(x):
    return lax.rsqrt(jnp.mean(x * x, axis=1, keepdims=True) + EPSILON)


def kernel(
    acts_hbm, saved_hbm, ograd_hbm, kept_hbm, lens_hbm, wq_hbm, wkv_hbm, wo_hbm,
    handed_out, back_out, gq_out, gkv_out, go_out,
    acts, saved, ograd, kept, lens, buf, wq, wkv, wkv_pairs, wo, kept2, lens2, normed, raw, picked, chosen, stash, part, sibrecv, chip, yrecv, hsrc, hrecv,
    tiles, handed, back, gq, gkv, go,
    wsem, osem, dps, dpr, ags, agr, r1s, r1r, r2s, r2r, hs, hr,
):
    pipes = lax.axis_size("pipe")
    p, r, t = lax.axis_index("pipe"), lax.axis_index("dp"), lax.axis_index("tensor")
    y, c = t // 2, t % 2
    own = c * 4 + y
    first, last = p == 0, p == pipes - 1
    inner = jnp.logical_not(first | last)
    width = wq.shape[0]
    real_rows = acts.shape[0] * HEAD // (2 * width)
    keep = kept.shape[3]
    half_width, packed, quarter = width // 2, 3 * width // 4, width // 4
    next_pipe = {"pipe": lax.rem(p + 1, pipes)}
    prev_pipe = {"pipe": lax.rem(p + pipes - 1, pipes)}
    sibling = {"tensor": y * 2 + 1 - c}
    other_dp = {"dp": 1 - r}

    def peer_y(d):
        return lax.rem(y + d, 4)

    def remote(src, dst, send, recv, device):
        return pltpu.make_async_remote_copy(
            src_ref=src, dst_ref=dst, send_sem=send, recv_sem=recv, device_id=device, device_id_type=MESH
        )

    barrier = pltpu.get_barrier_semaphore()
    greet = [{"tensor": lax.rem(t + d, 8)} for d in range(1, 8)] + [other_dp, next_pipe, prev_pipe]
    for device in greet:
        pl.semaphore_signal(barrier, inc=1, device_id=device, device_id_type=MESH)

    loads = [
        pltpu.make_async_copy(src, dst, wsem.at[i])
        for i, (src, dst) in enumerate(
            (
                (saved_hbm, saved),
                (ograd_hbm, ograd),
                (acts_hbm, acts),
                (kept_hbm, kept),
                (lens_hbm, lens),
                (wkv_hbm, wkv_pairs),
                (wq_hbm.at[0], wq),
                (wo_hbm.at[0], wo),
            )
        )
    ]
    for load in loads:
        load.start()
    stores = [
        pltpu.make_async_copy(src, dst, osem.at[i])
        for i, (src, dst) in enumerate(
            ((handed, handed_out), (back, back_out), (gq, gq_out), (gkv, gkv_out), (go, go_out))
        )
    ]
    tiles[...] = jnp.zeros_like(tiles)

    lines = acts.shape[0]
    q, k = iota((lines, lines), 0), iota((lines, lines), 1)
    spread = jnp.where(line_of(q, width) == k, 1.0, 0.0).astype(BF16)
    for load in loads[:5]:
        load.wait()
    rows = nn(spread, jnp.concatenate([saved[...], ograd[...], acts[...]], axis=1)).astype(BF16)
    for ct in range(packed // HEAD):
        for slot in range(2):
            for arr in (SAVED, GRAD, ACTS):
                at = (2 * ct + slot) * ROWS_PAD
                buf[arr, slot, own, :, ct * HEAD : (ct + 1) * HEAD] = rows[
                    at : at + ROWS_PAD, arr * HEAD : (arr + 1) * HEAD
                ]

    pl.semaphore_wait(barrier, len(greet))

    def dp_copy(arr, slot):
        return remote(
            buf.at[arr, slot, own], buf.at[arr + 3, slot, own],
            dps.at[arr, slot], dpr.at[arr, slot], other_dp,
        )

    kept_copy = remote(kept.at[0, 0], kept2, dps.at[2, 0], dpr.at[2, 0], other_dp)
    lens_copy = remote(lens.at[0, 0], lens2, dps.at[2, 1], dpr.at[2, 1], other_dp)

    def slab_to(arr, slot, slab, sem, device):
        here = buf.at[arr, slot, slab]
        return remote(here, here, ags.at[arr, slot, sem], agr.at[arr, slot, slab], device)

    def across(sem, slab, arr, slot, d):
        slab_to(arr, slot, slab, sem, {"tensor": peer_y(d) * 2 + c}).start()

    def ag_take(arr, slot, d):
        copy = slab_to(arr, slot, c * 4 + peer_y(d), 3 + d, sibling)
        copy.wait_recv()
        copy.start()

    def ag_rest(arr, slot):
        ag_take(arr, slot, 1 if (arr + slot) % 2 == 0 else 3)
        ag_take(arr, slot, 2)

    def ag_wait(arr, slot):
        for d in range(4):
            slab_to(arr, slot, (1 - c) * 4 + peer_y(d), 3, sibling).wait_recv()

    def ag_end(arr, slot):
        for d in range(7):
            slab_to(arr, slot, own, d, sibling).wait_send()

    def split_weights():
        loads[5].wait()
        apart = pairs_apart()

        def split(i, carry):
            two = pl.multiple_of(i * 512, 512)
            pairs = jnp.concatenate(
                [wkv_pairs[pl.ds(two, 256), :], wkv_pairs[pl.ds(two + 256, 256), :]], axis=1
            )
            got = nn(apart, pairs).astype(BF16)
            for j in range(2):
                at = pl.ds(pl.multiple_of(i * 256 + j * 128, 128), 128)
                cols = slice(j * HEAD, (j + 1) * HEAD)
                wkv[at, 0:HEAD] = got[:HEAD, cols]
                wkv[at, HEAD:] = got[HEAD:, cols]
            return carry

        lax.fori_loop(0, width // 256, split, 0)
        for load in loads[6:]:
            load.wait()

    def slab_rows(i):
        return pl.ds(pl.multiple_of(i * ROWS_PAD, ROWS_PAD), ROWS_PAD)

    def for_slabs(slabs, step):
        lax.fori_loop(0, slabs, lambda i, carry: step(i) or carry, 0, unroll=2)

    def received(arr, i):
        return unpack(buf[arr, i // SLABS, i % SLABS].astype(F32))

    def to_raw(arr, slabs):
        def step(i):
            raw[arr, slab_rows(i), :] = received(arr, i).astype(BF16)

        for_slabs(slabs, step)

    def normalise(which, slab_of, slabs):
        def step(i):
            x = slab_of(i)
            normed[which, slab_rows(i), :] = (x * inverse_root(x)).astype(BF16)

        for_slabs(slabs, step)

    def places(kept_list, lengths, rows):
        pos_col = kept_positions(kept_list, real_rows)
        pos_row = to_row(pos_col)
        if rows > HALF_ROWS:
            more = dropped_positions(kept_list, real_rows)
            pos_row = jnp.concatenate([pos_row, more], axis=1)
            pos_col = jnp.concatenate([pos_col, to_col(more)], axis=0)
        allowed = (document_of(pos_col, lengths) == document_of(pos_row, lengths)) & (
            pos_row <= pos_col
        )
        return pos_col, allowed

    def heads(which, rows, allowed):
        x = normed[which, 0:rows, :]
        queries = nn(x, wq[...]).astype(BF16)
        keyval = nn(x, wkv[...]).astype(BF16)
        keys, values = keyval[:, :HEAD], keyval[:, HEAD:]
        out = []
        for h in range(2):
            q = queries[:, h * HEAD : (h + 1) * HEAD]
            scores = jnp.where(allowed, nt(q, keys) * HEAD ** (-0.5), -jnp.inf)
            e = jnp.exp(scores - jnp.max(scores, axis=1, keepdims=True))
            probs = e / jnp.sum(e, axis=1, keepdims=True)
            rounded = probs.astype(BF16)
            out.append((q, probs, rounded, nn(rounded, values).astype(BF16)))
        return keys, values, out

    def store_part(f, rows, term):
        packs = pack([term(i * quarter) for i in range(3)], term(3 * quarter))
        for i, value in enumerate(packs):
            value = value.astype(BF16)
            for slot in range(rows // HALF_ROWS):
                part[f, slot, :, :, i * quarter : (i + 1) * quarter] = value[
                    slot * HALF_ROWS : (slot + 1) * HALF_ROWS
                ].reshape(SLABS, ROWS_PAD, quarter)

    def run_forward(rows, allowed):
        _, _, out = heads(2, rows, allowed)
        mixed = jnp.concatenate([o[3] for o in out], axis=1)
        store_part(FORWARD, rows, lambda n0: nn(mixed, wo[:, n0 : n0 + quarter]))

    def run_back(which, rows, pos_col, allowed, middle, late):
        keys, values, out = heads(which, rows, allowed)
        middle()
        to_raw(GRAD + 3 * which, rows // ROWS_PAD)
        upstream = raw[GRAD + 3 * which, 0:rows, :]
        grad_mixed = nt(upstream, wo[...]).astype(BF16)
        mixed = jnp.concatenate([o[3] for o in out], axis=1)
        if rows > HALF_ROWS:
            picks = select(pos_col, real_rows, keep)
            grad_mixed = nn(picks, grad_mixed).astype(BF16)
            mixed = tn(picks, mixed).astype(BF16)
            if which == 0:
                chosen[...] = picks
        grad_k = jnp.zeros((rows, HEAD), F32)
        grad_v = jnp.zeros((rows, HEAD), F32)
        grad_q = []
        for h, (q, probs, rounded, _) in enumerate(out):
            gm = grad_mixed[:, h * HEAD : (h + 1) * HEAD]
            grad_probs = nt(gm, values)
            centre = jnp.sum(probs * grad_probs, axis=1, keepdims=True)
            scores = (probs * (grad_probs - centre) * HEAD ** (-0.5)).astype(BF16)
            grad_q.append(nn(scores, keys).astype(BF16))
            grad_k = grad_k + tn(scores, q)
            grad_v = grad_v + tn(rounded, gm)
        gq_rows = jnp.concatenate(grad_q, axis=1)
        gkv_rows = jnp.concatenate([grad_k.astype(BF16), grad_v.astype(BF16)], axis=1)
        stash[which, 0, 0:rows, :] = gq_rows
        stash[which, 1, 0:rows, :] = gkv_rows
        stash[which, 2, 0:rows, :] = mixed
        late()
        if which == 0:
            store_part(
                BACK,
                rows,
                lambda n0: nt(gq_rows, wq[n0 : n0 + quarter, :]) + nt(gkv_rows, wkv[n0 : n0 + quarter, :]),
            )

    def rs1(f, slot):
        return remote(
            part.at[f, slot, pl.ds((1 - c) * 4, 4)], sibrecv.at[f, slot],
            r1s.at[f, slot], r1r.at[f, slot], sibling,
        )

    def rs_send(f, slot):
        rs1(f, slot).start()

    def rs2(f, slot, d):
        return remote(
            chip.at[f, slot, peer_y(d)], yrecv.at[f, slot, y],
            r2s.at[f, slot, d - 1], r2r.at[f, slot, y], {"tensor": peer_y(d) * 2 + c},
        )

    def rs_cross(f, slot):
        rs1(f, slot).wait_recv()
        for d in (2, 1, 3):
            there = peer_y(d)
            total = part[f, slot, c * 4 + there].astype(F32) + sibrecv[f, slot, there].astype(F32)
            chip[f, slot, there] = total.astype(BF16)
            rs2(f, slot, d).start()

    def rs_total(f, slot):
        total = part[f, slot, own].astype(F32) + sibrecv[f, slot, y].astype(F32)
        for d in (1, 3, 2):
            there = peer_y(d)
            here = yrecv.at[f, slot, there]
            remote(here, here, r2s.at[f, slot, d - 1], r2r.at[f, slot, there], sibling).wait_recv()
            total = total + yrecv[f, slot, there].astype(F32)
        return unpack(total)

    def rs_end(f, slot):
        rs1(f, slot).wait_send()
        for d in (1, 2, 3):
            rs2(f, slot, d).wait_send()

    def hand(f, slot, device):
        return remote(hsrc.at[f, slot], hrecv.at[f, slot], hs.at[f, slot], hr.at[f, slot], device)

    columns = pl.ds(pl.multiple_of(r * half_width, half_width), half_width)

    def weights(rows):
        def stashed(which, i):
            return stash[which, i, 0:rows, :]

        def ups(which):
            return raw[GRAD + 3 * which, 0:rows, columns]

        x0, x1 = normed[0, 0:rows, columns], normed[1, 0:rows, columns]
        go[...] = (tn(stashed(0, 2), ups(0)) + tn(stashed(1, 2), ups(1))).astype(BF16)
        stores[4].start()
        gq[...] = (tn(x0, stashed(0, 0)) + tn(x1, stashed(1, 0))).astype(BF16)
        stores[2].start()
        both = (tn(x0, stashed(0, 1)) + tn(x1, stashed(1, 1))).astype(BF16)
        joined = jnp.transpose(pairs_apart().astype(F32)).astype(BF16)
        for i in range(half_width // HEAD):
            block = both[i * HEAD : (i + 1) * HEAD]
            block = jnp.concatenate([block[:, :HEAD], block[:, HEAD:]], axis=0)
            gkv[i * 256 : (i + 1) * 256, :] = nn(joined, block).astype(BF16)
        stores[3].start()

    def section(at_first, at_last):
        rows = 2 * HALF_ROWS if at_last else HALF_ROWS
        ends = at_first or at_last

        def slots_of(arr, action):
            two = at_last or (at_first and arr not in (GRAD, GRAD_2))
            for slot in range(2 if two else 1):
                action(arr, slot)

        def slots_rs(f, action):
            for slot in (1, 0) if at_last else (0,):
                action(f, slot)

        def direct(arr):
            return not ends or (at_first and arr in (SAVED_2, GRAD_2))

        def ag_start(arr, slot):
            if direct(arr):
                across(1, own, arr, slot, 2)
            across(0, own, arr, slot, 1)
            across(2, own, arr, slot, 3)
            slab_to(arr, slot, own, 3, sibling).start()

        def ag_near(arr, slot):
            source, target = (3, 1) if (arr + slot) % 2 == 0 else (1, 3)
            ag_take(arr, slot, source)
            if not direct(arr):
                across(1, c * 4 + peer_y(source), arr, slot, target)

        def near(*arrs):
            for arr in arrs:
                slots_of(arr, ag_near)

        def rest(*arrs):
            for arr in arrs:
                slots_of(arr, ag_rest)

        def relay():
            def one(arr, slot):
                dp_copy(arr, slot).wait_recv()
                ag_start(arr + 3, slot)

            slots_of(SAVED, one)
            slots_of(GRAD, one)

        def prepare(arr, which, pos_col):
            slots_of(arr, ag_wait)
            if at_first:
                to_raw(arr, 2 * SLABS)
                picks = select(pos_col, real_rows, keep)
                for n0 in range(0, width, quarter):
                    picked[which, :, n0 : n0 + quarter] = nn(
                        picks, raw[arr, :, n0 : n0 + quarter]
                    ).astype(BF16)
                normalise(which, lambda i: picked[which, slab_rows(i), :].astype(F32), SLABS)
            else:
                normalise(which, lambda i: received(arr, i), rows // ROWS_PAD)

        def finish_back(f, slot):
            total = rs_total(f, slot)
            at = slot * SLABS + own
            x = picked[0, slab_rows(own), :].astype(F32) if at_first else received(SAVED, at)
            if at_last:
                g = nn(chosen[slab_rows(at), :], raw[GRAD])
            else:
                g = raw[GRAD, slab_rows(own), :].astype(F32)
            scale = inverse_root(x)
            unrounded = x * scale
            inner_mean = jnp.mean(total * unrounded, axis=1, keepdims=True)
            hsrc[f, slot] = pack_slab(g + scale * (total - unrounded * inner_mean)).astype(BF16)
            if slot == 1:
                hand(f, 1, next_pipe).start()
            elif not at_first:
                hand(f, 0, prev_pipe).start()

        def finish_forward(f, slot):
            total = rs_total(f, slot)
            x = picked[2, slab_rows(own), :].astype(F32) if at_first else received(ACTS, slot * SLABS + own)
            hsrc[f, slot] = pack_slab(x + total).astype(BF16)
            if not at_last:
                hand(f, 0, next_pipe).start()

        def nothing():
            pass

        slots_of(SAVED, lambda arr, slot: dp_copy(arr, slot).start())
        slots_of(GRAD, lambda arr, slot: dp_copy(arr, slot).start())
        kept_copy.start()
        lens_copy.start()
        for arr in (SAVED, GRAD) if at_last else (ACTS, SAVED, GRAD):
            slots_of(arr, ag_start)
        split_weights()
        pos_fwd, allowed_fwd = places(kept[0, 0, 0:1, :].astype(F32), lens[0, 0, 0:1, :].astype(F32), rows)
        pos_back, allowed_back = places(kept[0, 0, 1:2, :].astype(F32), lens[0, 0, 1:2, :].astype(F32), rows)

        if at_last:
            near(SAVED, GRAD)
            slots_of(ACTS, ag_start)
            rest(SAVED, GRAD)
            prepare(SAVED, 0, pos_back)

            def middle():
                near(ACTS)
                slots_of(GRAD, ag_wait)

            run_back(0, rows, pos_back, allowed_back, middle, lambda: rest(ACTS))
            slots_rs(BACK, rs_send)
            slots_rs(BACK, rs_cross)
            relay()
            prepare(ACTS, 2, pos_fwd)
            slots_rs(BACK, finish_back)
            near(SAVED_2, GRAD_2)
            run_forward(rows, allowed_fwd)
            slots_rs(FORWARD, rs_send)
            rest(SAVED_2, GRAD_2)
            slots_rs(FORWARD, rs_cross)
        else:
            near(ACTS)
            if at_first:
                near(SAVED, GRAD)
            rest(ACTS)
            prepare(ACTS, 2, pos_fwd)
            if at_first:
                drop_row = dropped_positions(kept[0, 0, 0:1, :].astype(F32), real_rows)
                mine = iota((ROWS_PAD, HALF_ROWS), 1) == own * ROWS_PAD + iota((ROWS_PAD, HALF_ROWS), 0)
                drop_col = jnp.sum(jnp.where(mine, drop_row, 0.0), axis=1, keepdims=True)
                hsrc[FORWARD, 1] = pack_slab(nn(select(drop_col, real_rows, keep), raw[ACTS])).astype(BF16)
                hand(FORWARD, 1, prev_pipe).start()
            run_forward(rows, allowed_fwd)
            slots_rs(FORWARD, rs_send)
            if not at_first:
                near(SAVED, GRAD)
            rest(SAVED, GRAD)
            slots_rs(FORWARD, rs_cross)
            prepare(SAVED, 0, pos_back)
            if at_first:
                relay()
            run_back(0, rows, pos_back, allowed_back, lambda: slots_of(GRAD, ag_wait), nothing)
            slots_rs(BACK, rs_send)
            slots_rs(FORWARD, finish_forward)
            if not at_first:
                slots_rs(BACK, rs_cross)
                relay()
                slots_rs(BACK, finish_back)
            near(SAVED_2, GRAD_2)
            rest(SAVED_2, GRAD_2)
            if at_first:
                slots_rs(BACK, rs_cross)

        kept_copy.wait_recv()
        lens_copy.wait_recv()
        pos_two, allowed_two = places(kept2[1:2, :].astype(F32), lens2[1:2, :].astype(F32), rows)
        prepare(SAVED_2, 1, pos_two)
        run_back(1, rows, pos_two, allowed_two, lambda: slots_of(GRAD_2, ag_wait), nothing)
        if at_last:
            slots_rs(FORWARD, finish_forward)
        if at_first:
            slots_rs(BACK, finish_back)
        weights(rows)

        for f, none, two in ((FORWARD, at_first, at_last), (BACK, at_last, at_first)):
            for slot in ([] if none else [0]) + ([1] if two else []):
                hand(f, slot, next_pipe).wait_recv()
                for ct in range(packed // HEAD):
                    at = (2 * ct + slot) * ROWS_PAD
                    tiles[at : at + ROWS_PAD, f * HEAD : (f + 1) * HEAD] = hrecv[
                        f, slot, :, ct * HEAD : (ct + 1) * HEAD
                    ]
        q, k = iota((lines, lines), 1), iota((lines, lines), 0)
        gather = jnp.where(line_of(q, width) == k, 1.0, 0.0).astype(BF16)
        found = nn(gather, tiles[...]).astype(BF16)
        handed[...] = found[:, FORWARD * HEAD : (FORWARD + 1) * HEAD]
        back[...] = found[:, BACK * HEAD : (BACK + 1) * HEAD]
        stores[0].start()
        stores[1].start()

        for arr in range(5):
            slots_of(arr, ag_end)
        for arr in (SAVED, GRAD):
            slots_of(arr, lambda arr, slot: dp_copy(arr, slot).wait_send())
        kept_copy.wait_send()
        lens_copy.wait_send()
        for f in (BACK, FORWARD):
            slots_rs(f, rs_end)
        if not at_last:
            hand(FORWARD, 0, next_pipe).wait_send()
        if not at_first:
            hand(BACK, 0, next_pipe).wait_send()
        if at_first:
            hand(FORWARD, 1, next_pipe).wait_send()
        if at_last:
            hand(BACK, 1, next_pipe).wait_send()
        for store in stores:
            store.wait()

    pl.when(inner)(lambda: section(False, False))
    pl.when(first)(lambda: section(True, False))
    pl.when(last)(lambda: section(False, True))


def copy_kernel(*refs):
    ins, outs, held, load, store = refs[:5], refs[5:10], refs[10:15], refs[15], refs[16]
    loads = [pltpu.make_async_copy(ins[i], held[i], load.at[i]) for i in range(5)]
    stores = [pltpu.make_async_copy(held[i], outs[i], store.at[i]) for i in range(5)]
    for copy in loads:
        copy.start()
    for i in range(5):
        loads[i].wait()
        stores[i].start()
    for copy in stores:
        copy.wait()


def lines_of(x):
    _, _, slots, rows, width = x.shape
    x = x.reshape(slots, rows, width // HEAD, HEAD)
    return jnp.transpose(x, (1, 2, 0, 3)).reshape(-1, HEAD)


def from_lines(x, shape):
    _, _, slots, rows, width = shape
    x = x.reshape(rows, width // HEAD, slots, HEAD)
    return jnp.transpose(x, (2, 0, 1, 3)).reshape(shape)


def local(acts_in, saved_in, out_grad, w_query, w_keyval, w_out, kept_rows, doc_lengths):
    width = acts_in.shape[4]
    cols = w_query.shape[2]
    slab = (ROWS_PAD, 3 * width // 4)
    lines = 2 * acts_in.shape[3] * width // HEAD
    dma = pltpu.SemaphoreType.DMA
    anywhere = pl.BlockSpec(memory_space=pl.ANY)
    outs = ((lines, HEAD), (lines, HEAD), (width // 2, cols), (width, HEAD), (cols, width // 2))
    out_shape = tuple(jax.ShapeDtypeStruct(shape, BF16) for shape in outs)
    results = pl.pallas_call(
        kernel,
        out_shape=out_shape,
        in_specs=[anywhere] * 8,
        out_specs=[anywhere] * 5,
        scratch_shapes=[pltpu.VMEM((lines, HEAD), BF16)] * 3
        + [
            pltpu.VMEM(kept_rows.shape, jnp.int32),
            pltpu.VMEM(doc_lengths.shape, jnp.int32),
            pltpu.VMEM((5, 2, SLABS) + slab, BF16),
            pltpu.VMEM((width, cols), BF16),
            pltpu.VMEM((width, 2 * HEAD), BF16),
            pltpu.VMEM((2 * width, HEAD), BF16),
            pltpu.VMEM((cols, width), BF16),
            pltpu.VMEM(kept_rows.shape[2:], jnp.int32),
            pltpu.VMEM(doc_lengths.shape[2:], jnp.int32),
            pltpu.VMEM((3, 2 * HALF_ROWS, width), BF16),
            pltpu.VMEM((5, 2 * HALF_ROWS, width), BF16),
            pltpu.VMEM((3, HALF_ROWS, width), BF16),
            pltpu.VMEM((2 * HALF_ROWS, 2 * HALF_ROWS), BF16),
            pltpu.VMEM((2, 3, 2 * HALF_ROWS, 2 * HEAD), BF16),
            pltpu.VMEM((2, 2, SLABS) + slab, BF16),
            pltpu.VMEM((2, 2, 4) + slab, BF16),
            pltpu.VMEM((2, 2, 4) + slab, BF16),
            pltpu.VMEM((2, 2, 4) + slab, BF16),
            pltpu.VMEM((2, 2) + slab, BF16),
            pltpu.VMEM((2, 2) + slab, BF16),
            pltpu.VMEM((lines, 2 * HEAD), BF16),
        ]
        + [pltpu.VMEM(shape, BF16) for shape in outs]
        + [
            dma((8,)),
            dma((5,)),
            dma((3, 2)),
            dma((3, 2)),
            dma((5, 2, 7)),
            dma((5, 2, SLABS)),
            dma((2, 2)),
            dma((2, 2)),
            dma((2, 2, 3)),
            dma((2, 2, 4)),
            dma((2, 2)),
            dma((2, 2)),
        ],
        compiler_params=pltpu.CompilerParams(
            collective_id=0, has_side_effects=True, vmem_limit_bytes=56 * 1024 * 1024
        ),
        cost_estimate=pl.CostEstimate(flops=4_000_000_000, bytes_accessed=8_000_000, transcendentals=200_000),
        name="section",
    )(
        lines_of(acts_in), lines_of(saved_in), lines_of(out_grad), kept_rows, doc_lengths, w_query,
        w_keyval.reshape(2 * width, HEAD), w_out,
    )
    handed, back, gq, gkv, go = pl.pallas_call(
        copy_kernel,
        out_shape=out_shape,
        in_specs=[anywhere] * 5,
        out_specs=[anywhere] * 5,
        scratch_shapes=[pltpu.VMEM(shape, BF16) for shape in outs] + [dma((5,)), dma((5,))],
        cost_estimate=pl.CostEstimate(flops=0, bytes_accessed=4_000_000, transcendentals=0),
        name="results",
    )(*results)
    return (
        from_lines(handed, acts_in.shape),
        from_lines(back, acts_in.shape),
        gq[None],
        gkv.reshape(1, width // 2, 2, HEAD),
        go[None],
    )


def solution(mesh):
    placed = (
        P("pipe", "dp", None, "tensor", None),
        P("pipe", "dp", None, "tensor", None),
        P("pipe", "dp", None, "tensor", None),
        P("pipe", None, "tensor"),
        P("pipe", None, None, "tensor"),
        P("pipe", "tensor", None),
        P("pipe", "dp", None, None),
        P("pipe", "dp", None, None),
    )
    return jax.shard_map(
        local,
        mesh=mesh,
        in_specs=placed,
        out_specs=(
            P("pipe", "dp", None, "tensor", None),
            P("pipe", "dp", None, "tensor", None),
            P("pipe", "dp", "tensor"),
            P("pipe", "dp", None, "tensor"),
            P("pipe", "tensor", "dp"),
        ),
        check_vma=False,
    )
```

```python
import jax
import jax.numpy as jnp
from jax import lax
from jax.experimental import pallas as pl
from jax.experimental.pallas import tpu as pltpu
from jax.sharding import PartitionSpec as P

HEAD = 128
EPSILON = 1e-06
MESH = pl.DeviceIdType.MESH
F32 = jnp.float32
BF16 = jnp.bfloat16

SAVED, GRAD, ACTS, SAVED_2, GRAD_2 = range(5)
BACK, FORWARD = 0, 1
ROWS_PAD = 16
SLABS = 8
HALF_ROWS = SLABS * ROWS_PAD


def nn(a, b):
    return lax.dot_general(a, b, (((1,), (0,)), ((), ())), preferred_element_type=F32)


def nt(a, b):
    return lax.dot_general(a, b, (((1,), (1,)), ((), ())), preferred_element_type=F32)


def tn(a, b):
    return lax.dot_general(a, b, (((0,), (0,)), ((), ())), preferred_element_type=F32)


def iota(shape, dim):
    return lax.broadcasted_iota(jnp.int32, shape, dim)


def list_index(a, real_rows):
    core, y, r = a // 64, (a // 16) % 4, a % 16
    return (2 * y + core) * real_rows + r, r < real_rows


def to_row(col):
    n = col.shape[0]
    return jnp.sum(jnp.where(iota((n, n), 0) == iota((n, n), 1), col, 0.0), axis=0, keepdims=True)


def to_col(row):
    n = row.shape[1]
    return jnp.sum(jnp.where(iota((n, n), 0) == iota((n, n), 1), row, 0.0), axis=1, keepdims=True)


def kept_positions(kept, real_rows):
    keep = kept.shape[1]
    place, real = list_index(iota((HALF_ROWS, keep), 0), real_rows)
    hit = (place == iota((HALF_ROWS, keep), 1)) & real
    found = jnp.sum(jnp.where(hit, kept, 0.0), axis=1, keepdims=True)
    _, real_col = list_index(iota((HALF_ROWS, 1), 0), real_rows)
    return jnp.where(real_col, found, 1000.0)


def dropped_positions(kept, real_rows):
    keep = kept.shape[1]
    n = 256
    named = jnp.max(
        jnp.where(iota((n, keep), 0).astype(F32) == kept, 1.0, 0.0), axis=1, keepdims=True
    )
    free = jnp.where(iota((n, 1), 0) < 2 * keep, 1.0 - named, 0.0)
    count = jnp.sum(
        jnp.where(iota((n, n), 1) <= iota((n, n), 0), to_row(free), 0.0), axis=1, keepdims=True
    )
    place, real = list_index(iota((n, HALF_ROWS), 1), real_rows)
    hit = (count - 1.0 == place.astype(F32)) & (free > 0.5) & real
    found = jnp.sum(jnp.where(hit, iota((n, HALF_ROWS), 0).astype(F32), 0.0), axis=0, keepdims=True)
    _, real_row = list_index(iota((1, HALF_ROWS), 1), real_rows)
    return jnp.where(real_row, found, 1000.0)


def document_of(positions, lengths):
    bound = jnp.zeros((1, 1), F32)
    total = jnp.zeros(positions.shape, F32)
    for m in range(lengths.shape[1]):
        bound = bound + lengths[:, m : m + 1]
        total = total + jnp.where(positions >= bound, 1.0, 0.0)
    return total


def select(pos_col, real_rows, keep):
    n = 2 * HALF_ROWS
    b = iota((1, n), 1)
    place, real = list_index(b % HALF_ROWS, real_rows)
    flat = jnp.where(real, (b // HALF_ROWS) * keep + place, -1).astype(F32)
    return jnp.where(pos_col == flat, 1.0, 0.0).astype(BF16)


def line_of(q, width):
    tile, slot, r = q // (2 * ROWS_PAD), (q // ROWS_PAD) % 2, q % ROWS_PAD
    quarter = width // HEAD // 4
    spill = r >= 12
    row = jnp.where(spill, 4 * (tile // quarter) + r - 12, r)
    place = jnp.where(spill, 3 * quarter + tile % quarter, tile)
    return (row * (4 * quarter) + place) * 2 + slot


def unpack(x):
    w = x.shape[1] // 3
    r = iota((ROWS_PAD, 1), 0)
    tail = jnp.where(
        r < 4,
        pltpu.roll(x[:, :w], 4, 0),
        jnp.where(r < 8, pltpu.roll(x[:, w : 2 * w], 8, 0), pltpu.roll(x[:, 2 * w :], 12, 0)),
    )
    return jnp.where(r < 12, jnp.concatenate([x, tail], axis=1), 0.0)


def pack(parts, tail):
    r = iota((tail.shape[0], 1), 0) % ROWS_PAD
    return [jnp.where(r < 12, x, pltpu.roll(tail, 12 - 4 * i, 0)) for i, x in enumerate(parts)]


def pack_slab(x):
    w = x.shape[1] // 4
    return jnp.concatenate(pack([x[:, i * w : (i + 1) * w] for i in range(3)], x[:, 3 * w :]), axis=1)


def pairs_apart():
    n = 2 * HEAD
    q, k = iota((n, n), 0), iota((n, n), 1)
    return jnp.where((q % HEAD) * 2 + q // HEAD == k, 1.0, 0.0).astype(BF16)


def inverse_root(x):
    return lax.rsqrt(jnp.mean(x * x, axis=1, keepdims=True) + EPSILON)


def kernel(
    acts_hbm, saved_hbm, ograd_hbm, kept_hbm, lens_hbm, wq_hbm, wkv_hbm, wo_hbm,
    handed_out, back_out, gq_out, gkv_out, go_out,
    acts, saved, ograd, kept, lens, buf, wq, wkv, wkv_pairs, wo, kept2, lens2, normed, raw, picked, chosen, stash, part, sibrecv, chip, yrecv, hsrc, hrecv,
    tiles, handed, back, gq, gkv, go,
    wsem, osem, dps, dpr, ags, agr, r1s, r1r, r2s, r2r, hs, hr,
):
    pipes = lax.axis_size("pipe")
    p, r, t = lax.axis_index("pipe"), lax.axis_index("dp"), lax.axis_index("tensor")
    y, c = t // 2, t % 2
    own = c * 4 + y
    first, last = p == 0, p == pipes - 1
    inner = jnp.logical_not(first | last)
    width = wq.shape[0]
    real_rows = acts.shape[0] * HEAD // (2 * width)
    keep = kept.shape[3]
    half_width, packed, quarter = width // 2, 3 * width // 4, width // 4
    next_pipe = {"pipe": lax.rem(p + 1, pipes)}
    prev_pipe = {"pipe": lax.rem(p + pipes - 1, pipes)}
    sibling = {"tensor": y * 2 + 1 - c}
    other_dp = {"dp": 1 - r}

    def peer_y(d):
        return lax.rem(y + d, 4)

    def remote(src, dst, send, recv, device):
        return pltpu.make_async_remote_copy(
            src_ref=src, dst_ref=dst, send_sem=send, recv_sem=recv, device_id=device, device_id_type=MESH
        )

    barrier = pltpu.get_barrier_semaphore()
    greet = [{"tensor": lax.rem(t + d, 8)} for d in range(1, 8)] + [other_dp, next_pipe, prev_pipe]
    for device in greet:
        pl.semaphore_signal(barrier, inc=1, device_id=device, device_id_type=MESH)

    loads = [
        pltpu.make_async_copy(src, dst, wsem.at[i])
        for i, (src, dst) in enumerate(
            (
                (saved_hbm, saved),
                (ograd_hbm, ograd),
                (acts_hbm, acts),
                (kept_hbm, kept),
                (lens_hbm, lens),
                (wkv_hbm, wkv_pairs),
                (wq_hbm.at[0], wq),
                (wo_hbm.at[0], wo),
            )
        )
    ]
    for load in loads:
        load.start()
    stores = [
        pltpu.make_async_copy(src, dst, osem.at[i])
        for i, (src, dst) in enumerate(
            ((handed, handed_out), (back, back_out), (gq, gq_out), (gkv, gkv_out), (go, go_out))
        )
    ]
    tiles[...] = jnp.zeros_like(tiles)

    lines = acts.shape[0]
    q, k = iota((lines, lines), 0), iota((lines, lines), 1)
    spread = jnp.where(line_of(q, width) == k, 1.0, 0.0).astype(BF16)
    for load in loads[:5]:
        load.wait()
    rows = nn(spread, jnp.concatenate([saved[...], ograd[...], acts[...]], axis=1)).astype(BF16)
    for ct in range(packed // HEAD):
        for slot in range(2):
            for arr in (SAVED, GRAD, ACTS):
                at = (2 * ct + slot) * ROWS_PAD
                buf[arr, slot, own, :, ct * HEAD : (ct + 1) * HEAD] = rows[
                    at : at + ROWS_PAD, arr * HEAD : (arr + 1) * HEAD
                ]

    pl.semaphore_wait(barrier, len(greet))

    def dp_copy(arr, slot):
        return remote(
            buf.at[arr, slot, own], buf.at[arr + 3, slot, own],
            dps.at[arr, slot], dpr.at[arr, slot], other_dp,
        )

    kept_copy = remote(kept.at[0, 0], kept2, dps.at[2, 0], dpr.at[2, 0], other_dp)
    lens_copy = remote(lens.at[0, 0], lens2, dps.at[2, 1], dpr.at[2, 1], other_dp)

    def slab_to(arr, slot, slab, sem, device):
        here = buf.at[arr, slot, slab]
        return remote(here, here, ags.at[arr, slot, sem], agr.at[arr, slot, slab], device)

    def across(sem, slab, arr, slot, d):
        slab_to(arr, slot, slab, sem, {"tensor": peer_y(d) * 2 + c}).start()

    def ag_take(arr, slot, d):
        copy = slab_to(arr, slot, c * 4 + peer_y(d), 3 + d, sibling)
        copy.wait_recv()
        copy.start()

    def ag_rest(arr, slot):
        ag_take(arr, slot, 1 if (arr + slot) % 2 == 0 else 3)
        ag_take(arr, slot, 2)

    def ag_wait(arr, slot):
        for d in range(4):
            slab_to(arr, slot, (1 - c) * 4 + peer_y(d), 3, sibling).wait_recv()

    def ag_end(arr, slot):
        for d in range(7):
            slab_to(arr, slot, own, d, sibling).wait_send()

    def split_weights():
        loads[5].wait()
        apart = pairs_apart()

        def split(i, carry):
            two = pl.multiple_of(i * 512, 512)
            pairs = jnp.concatenate(
                [wkv_pairs[pl.ds(two, 256), :], wkv_pairs[pl.ds(two + 256, 256), :]], axis=1
            )
            got = nn(apart, pairs).astype(BF16)
            for j in range(2):
                at = pl.ds(pl.multiple_of(i * 256 + j * 128, 128), 128)
                cols = slice(j * HEAD, (j + 1) * HEAD)
                wkv[at, 0:HEAD] = got[:HEAD, cols]
                wkv[at, HEAD:] = got[HEAD:, cols]
            return carry

        lax.fori_loop(0, width // 256, split, 0)
        for load in loads[6:]:
            load.wait()

    def slab_rows(i):
        return pl.ds(pl.multiple_of(i * ROWS_PAD, ROWS_PAD), ROWS_PAD)

    def for_slabs(slabs, step):
        lax.fori_loop(0, slabs, lambda i, carry: step(i) or carry, 0, unroll=4)

    def received(arr, i):
        return unpack(buf[arr, i // SLABS, i % SLABS].astype(F32))

    def to_raw(arr, slabs):
        def step(i):
            raw[arr, slab_rows(i), :] = received(arr, i).astype(BF16)

        for_slabs(slabs, step)

    def normalise(which, slab_of, slabs):
        def step(i):
            x = slab_of(i)
            normed[which, slab_rows(i), :] = (x * inverse_root(x)).astype(BF16)

        for_slabs(slabs, step)

    def places(kept_list, lengths, rows):
        pos_col = kept_positions(kept_list, real_rows)
        pos_row = to_row(pos_col)
        if rows > HALF_ROWS:
            more = dropped_positions(kept_list, real_rows)
            pos_row = jnp.concatenate([pos_row, more], axis=1)
            pos_col = jnp.concatenate([pos_col, to_col(more)], axis=0)
        allowed = (document_of(pos_col, lengths) == document_of(pos_row, lengths)) & (
            pos_row <= pos_col
        )
        return pos_col, allowed

    def heads(which, rows, allowed):
        x = normed[which, 0:rows, :]
        queries = nn(x, wq[...]).astype(BF16)
        keyval = nn(x, wkv[...]).astype(BF16)
        keys, values = keyval[:, :HEAD], keyval[:, HEAD:]
        out = []
        for h in range(2):
            q = queries[:, h * HEAD : (h + 1) * HEAD]
            scores = jnp.where(allowed, nt(q, keys) * HEAD ** (-0.5), -jnp.inf)
            e = jnp.exp(scores - jnp.max(scores, axis=1, keepdims=True))
            probs = e / jnp.sum(e, axis=1, keepdims=True)
            rounded = probs.astype(BF16)
            out.append((q, probs, rounded, nn(rounded, values).astype(BF16)))
        return keys, values, out

    def store_part(f, rows, term):
        packs = pack([term(i * quarter) for i in range(3)], term(3 * quarter))
        for i, value in enumerate(packs):
            value = value.astype(BF16)
            for slot in range(rows // HALF_ROWS):
                part[f, slot, :, :, i * quarter : (i + 1) * quarter] = value[
                    slot * HALF_ROWS : (slot + 1) * HALF_ROWS
                ].reshape(SLABS, ROWS_PAD, quarter)

    def run_forward(rows, allowed):
        _, _, out = heads(2, rows, allowed)
        mixed = jnp.concatenate([o[3] for o in out], axis=1)
        store_part(FORWARD, rows, lambda n0: nn(mixed, wo[:, n0 : n0 + quarter]))

    def run_back(which, rows, pos_col, allowed, middle, late):
        keys, values, out = heads(which, rows, allowed)
        middle()
        to_raw(GRAD + 3 * which, rows // ROWS_PAD)
        upstream = raw[GRAD + 3 * which, 0:rows, :]
        grad_mixed = nt(upstream, wo[...]).astype(BF16)
        mixed = jnp.concatenate([o[3] for o in out], axis=1)
        if rows > HALF_ROWS:
            picks = select(pos_col, real_rows, keep)
            grad_mixed = nn(picks, grad_mixed).astype(BF16)
            mixed = tn(picks, mixed).astype(BF16)
            if which == 0:
                chosen[...] = picks
        grad_k = jnp.zeros((rows, HEAD), F32)
        grad_v = jnp.zeros((rows, HEAD), F32)
        grad_q = []
        for h, (q, probs, rounded, _) in enumerate(out):
            gm = grad_mixed[:, h * HEAD : (h + 1) * HEAD]
            grad_probs = nt(gm, values)
            centre = jnp.sum(probs * grad_probs, axis=1, keepdims=True)
            scores = (probs * (grad_probs - centre) * HEAD ** (-0.5)).astype(BF16)
            grad_q.append(nn(scores, keys).astype(BF16))
            grad_k = grad_k + tn(scores, q)
            grad_v = grad_v + tn(rounded, gm)
        gq_rows = jnp.concatenate(grad_q, axis=1)
        gkv_rows = jnp.concatenate([grad_k.astype(BF16), grad_v.astype(BF16)], axis=1)
        stash[which, 0, 0:rows, :] = gq_rows
        stash[which, 1, 0:rows, :] = gkv_rows
        stash[which, 2, 0:rows, :] = mixed
        late()
        if which == 0:
            store_part(
                BACK,
                rows,
                lambda n0: nt(gq_rows, wq[n0 : n0 + quarter, :]) + nt(gkv_rows, wkv[n0 : n0 + quarter, :]),
            )

    def rs1(f, slot):
        return remote(
            part.at[f, slot, pl.ds((1 - c) * 4, 4)], sibrecv.at[f, slot],
            r1s.at[f, slot], r1r.at[f, slot], sibling,
        )

    def rs_send(f, slot):
        rs1(f, slot).start()

    def rs2(f, slot, d):
        return remote(
            chip.at[f, slot, peer_y(d)], yrecv.at[f, slot, y],
            r2s.at[f, slot, d - 1], r2r.at[f, slot, y], {"tensor": peer_y(d) * 2 + c},
        )

    def rs_cross(f, slot):
        rs1(f, slot).wait_recv()
        for d in (2, 1, 3):
            there = peer_y(d)
            total = part[f, slot, c * 4 + there].astype(F32) + sibrecv[f, slot, there].astype(F32)
            chip[f, slot, there] = total.astype(BF16)
            rs2(f, slot, d).start()

    def rs_total(f, slot):
        total = part[f, slot, own].astype(F32) + sibrecv[f, slot, y].astype(F32)
        for d in (1, 3, 2):
            there = peer_y(d)
            here = yrecv.at[f, slot, there]
            remote(here, here, r2s.at[f, slot, d - 1], r2r.at[f, slot, there], sibling).wait_recv()
            total = total + yrecv[f, slot, there].astype(F32)
        return unpack(total)

    def rs_end(f, slot):
        rs1(f, slot).wait_send()
        for d in (1, 2, 3):
            rs2(f, slot, d).wait_send()

    def hand(f, slot, device):
        return remote(hsrc.at[f, slot], hrecv.at[f, slot], hs.at[f, slot], hr.at[f, slot], device)

    columns = pl.ds(pl.multiple_of(r * half_width, half_width), half_width)

    def weights(rows):
        def stashed(which, i):
            return stash[which, i, 0:rows, :]

        def ups(which):
            return raw[GRAD + 3 * which, 0:rows, columns]

        x0, x1 = normed[0, 0:rows, columns], normed[1, 0:rows, columns]
        go[...] = (tn(stashed(0, 2), ups(0)) + tn(stashed(1, 2), ups(1))).astype(BF16)
        stores[4].start()
        gq[...] = (tn(x0, stashed(0, 0)) + tn(x1, stashed(1, 0))).astype(BF16)
        stores[2].start()
        both = (tn(x0, stashed(0, 1)) + tn(x1, stashed(1, 1))).astype(BF16)
        joined = jnp.transpose(pairs_apart().astype(F32)).astype(BF16)
        for i in range(half_width // HEAD):
            block = both[i * HEAD : (i + 1) * HEAD]
            block = jnp.concatenate([block[:, :HEAD], block[:, HEAD:]], axis=0)
            gkv[i * 256 : (i + 1) * 256, :] = nn(joined, block).astype(BF16)
        stores[3].start()

    def section(at_first, at_last):
        rows = 2 * HALF_ROWS if at_last else HALF_ROWS
        ends = at_first or at_last

        def slots_of(arr, action):
            two = at_last or (at_first and arr not in (GRAD, GRAD_2))
            for slot in range(2 if two else 1):
                action(arr, slot)

        def slots_rs(f, action):
            for slot in (1, 0) if at_last else (0,):
                action(f, slot)

        def direct(arr):
            return not ends or (at_first and arr in (SAVED_2, GRAD_2))

        def ag_start(arr, slot):
            if direct(arr):
                across(1, own, arr, slot, 2)
            across(0, own, arr, slot, 1)
            across(2, own, arr, slot, 3)
            slab_to(arr, slot, own, 3, sibling).start()

        def ag_near(arr, slot):
            source, target = (3, 1) if (arr + slot) % 2 == 0 else (1, 3)
            ag_take(arr, slot, source)
            if not direct(arr):
                across(1, c * 4 + peer_y(source), arr, slot, target)

        def near(*arrs):
            for arr in arrs:
                slots_of(arr, ag_near)

        def rest(*arrs):
            for arr in arrs:
                slots_of(arr, ag_rest)

        def relay():
            def one(arr, slot):
                dp_copy(arr, slot).wait_recv()
                ag_start(arr + 3, slot)

            slots_of(SAVED, one)
            slots_of(GRAD, one)

        def prepare(arr, which, pos_col):
            slots_of(arr, ag_wait)
            if at_first:
                to_raw(arr, 2 * SLABS)
                picks = select(pos_col, real_rows, keep)
                for n0 in range(0, width, quarter):
                    picked[which, :, n0 : n0 + quarter] = nn(
                        picks, raw[arr, :, n0 : n0 + quarter]
                    ).astype(BF16)
                normalise(which, lambda i: picked[which, slab_rows(i), :].astype(F32), SLABS)
            else:
                normalise(which, lambda i: received(arr, i), rows // ROWS_PAD)

        def finish_back(f, slot):
            total = rs_total(f, slot)
            at = slot * SLABS + own
            x = picked[0, slab_rows(own), :].astype(F32) if at_first else received(SAVED, at)
            if at_last:
                g = nn(chosen[slab_rows(at), :], raw[GRAD])
            else:
                g = raw[GRAD, slab_rows(own), :].astype(F32)
            scale = inverse_root(x)
            unrounded = x * scale
            inner_mean = jnp.mean(total * unrounded, axis=1, keepdims=True)
            hsrc[f, slot] = pack_slab(g + scale * (total - unrounded * inner_mean)).astype(BF16)
            if slot == 1:
                hand(f, 1, next_pipe).start()
            elif not at_first:
                hand(f, 0, prev_pipe).start()

        def finish_forward(f, slot):
            total = rs_total(f, slot)
            x = picked[2, slab_rows(own), :].astype(F32) if at_first else received(ACTS, slot * SLABS + own)
            hsrc[f, slot] = pack_slab(x + total).astype(BF16)
            if not at_last:
                hand(f, 0, next_pipe).start()

        def nothing():
            pass

        slots_of(SAVED, lambda arr, slot: dp_copy(arr, slot).start())
        slots_of(GRAD, lambda arr, slot: dp_copy(arr, slot).start())
        kept_copy.start()
        lens_copy.start()
        for arr in (SAVED, GRAD) if at_last else (ACTS, SAVED, GRAD):
            slots_of(arr, ag_start)
        split_weights()
        pos_fwd, allowed_fwd = places(kept[0, 0, 0:1, :].astype(F32), lens[0, 0, 0:1, :].astype(F32), rows)
        pos_back, allowed_back = places(kept[0, 0, 1:2, :].astype(F32), lens[0, 0, 1:2, :].astype(F32), rows)

        if at_last:
            near(SAVED, GRAD)
            slots_of(ACTS, ag_start)
            rest(SAVED, GRAD)
            prepare(SAVED, 0, pos_back)

            def middle():
                near(ACTS)
                slots_of(GRAD, ag_wait)

            def late():
                rest(ACTS)
                relay()

            run_back(0, rows, pos_back, allowed_back, middle, late)
            slots_rs(BACK, rs_send)
            slots_rs(BACK, rs_cross)
            prepare(ACTS, 2, pos_fwd)
            slots_rs(BACK, finish_back)
            near(SAVED_2, GRAD_2)
            run_forward(rows, allowed_fwd)
            slots_rs(FORWARD, rs_send)
            rest(SAVED_2, GRAD_2)
            slots_rs(FORWARD, rs_cross)
        else:
            near(ACTS)
            if at_first:
                near(SAVED, GRAD)
            rest(ACTS)
            prepare(ACTS, 2, pos_fwd)
            if at_first:
                drop_row = dropped_positions(kept[0, 0, 0:1, :].astype(F32), real_rows)
                mine = iota((ROWS_PAD, HALF_ROWS), 1) == own * ROWS_PAD + iota((ROWS_PAD, HALF_ROWS), 0)
                drop_col = jnp.sum(jnp.where(mine, drop_row, 0.0), axis=1, keepdims=True)
                hsrc[FORWARD, 1] = pack_slab(nn(select(drop_col, real_rows, keep), raw[ACTS])).astype(BF16)
                hand(FORWARD, 1, prev_pipe).start()
            run_forward(rows, allowed_fwd)
            slots_rs(FORWARD, rs_send)
            if not at_first:
                near(SAVED, GRAD)
            rest(SAVED, GRAD)
            slots_rs(FORWARD, rs_cross)
            prepare(SAVED, 0, pos_back)
            if at_first:
                relay()
            run_back(0, rows, pos_back, allowed_back, lambda: slots_of(GRAD, ag_wait), nothing)
            slots_rs(BACK, rs_send)
            slots_rs(FORWARD, finish_forward)
            if not at_first:
                slots_rs(BACK, rs_cross)
                relay()
                slots_rs(BACK, finish_back)
            near(SAVED_2, GRAD_2)
            rest(SAVED_2, GRAD_2)
            if at_first:
                slots_rs(BACK, rs_cross)

        kept_copy.wait_recv()
        lens_copy.wait_recv()
        pos_two, allowed_two = places(kept2[1:2, :].astype(F32), lens2[1:2, :].astype(F32), rows)
        prepare(SAVED_2, 1, pos_two)
        run_back(1, rows, pos_two, allowed_two, lambda: slots_of(GRAD_2, ag_wait), nothing)
        if at_last:
            slots_rs(FORWARD, finish_forward)
        weights(rows)
        if at_first:
            slots_rs(BACK, finish_back)

        q, k = iota((lines, lines), 1), iota((lines, lines), 0)
        gather = jnp.where(line_of(q, width) == k, 1.0, 0.0).astype(BF16)

        for f, none, two in ((FORWARD, at_first, at_last), (BACK, at_last, at_first)):
            for slot in ([] if none else [0]) + ([1] if two else []):
                hand(f, slot, next_pipe).wait_recv()
                for ct in range(packed // HEAD):
                    at = (2 * ct + slot) * ROWS_PAD
                    tiles[at : at + ROWS_PAD, f * HEAD : (f + 1) * HEAD] = hrecv[
                        f, slot, :, ct * HEAD : (ct + 1) * HEAD
                    ]
        found = nn(gather, tiles[...]).astype(BF16)
        handed[...] = found[:, FORWARD * HEAD : (FORWARD + 1) * HEAD]
        back[...] = found[:, BACK * HEAD : (BACK + 1) * HEAD]
        stores[0].start()
        stores[1].start()

        for arr in range(5):
            slots_of(arr, ag_end)
        for arr in (SAVED, GRAD):
            slots_of(arr, lambda arr, slot: dp_copy(arr, slot).wait_send())
        kept_copy.wait_send()
        lens_copy.wait_send()
        for f in (BACK, FORWARD):
            slots_rs(f, rs_end)
        if not at_last:
            hand(FORWARD, 0, next_pipe).wait_send()
        if not at_first:
            hand(BACK, 0, next_pipe).wait_send()
        if at_first:
            hand(FORWARD, 1, next_pipe).wait_send()
        if at_last:
            hand(BACK, 1, next_pipe).wait_send()
        for store in stores:
            store.wait()

    pl.when(inner)(lambda: section(False, False))
    pl.when(first)(lambda: section(True, False))
    pl.when(last)(lambda: section(False, True))


def copy_kernel(*refs):
    ins, outs, held, load, store = refs[:5], refs[5:10], refs[10:15], refs[15], refs[16]
    loads = [pltpu.make_async_copy(ins[i], held[i], load.at[i]) for i in range(5)]
    stores = [pltpu.make_async_copy(held[i], outs[i], store.at[i]) for i in range(5)]
    for copy in loads:
        copy.start()
    for i in range(5):
        loads[i].wait()
        stores[i].start()
    for copy in stores:
        copy.wait()


def lines_of(x):
    _, _, slots, rows, width = x.shape
    x = x.reshape(slots, rows, width // HEAD, HEAD)
    return jnp.transpose(x, (1, 2, 0, 3)).reshape(-1, HEAD)


def from_lines(x, shape):
    _, _, slots, rows, width = shape
    x = x.reshape(rows, width // HEAD, slots, HEAD)
    return jnp.transpose(x, (2, 0, 1, 3)).reshape(shape)


def local(acts_in, saved_in, out_grad, w_query, w_keyval, w_out, kept_rows, doc_lengths):
    width = acts_in.shape[4]
    cols = w_query.shape[2]
    slab = (ROWS_PAD, 3 * width // 4)
    lines = 2 * acts_in.shape[3] * width // HEAD
    dma = pltpu.SemaphoreType.DMA
    anywhere = pl.BlockSpec(memory_space=pl.ANY)
    outs = ((lines, HEAD), (lines, HEAD), (width // 2, cols), (width, HEAD), (cols, width // 2))
    out_shape = tuple(jax.ShapeDtypeStruct(shape, BF16) for shape in outs)
    results = pl.pallas_call(
        kernel,
        out_shape=out_shape,
        in_specs=[anywhere] * 8,
        out_specs=[anywhere] * 5,
        scratch_shapes=[pltpu.VMEM((lines, HEAD), BF16)] * 3
        + [
            pltpu.VMEM(kept_rows.shape, jnp.int32),
            pltpu.VMEM(doc_lengths.shape, jnp.int32),
            pltpu.VMEM((5, 2, SLABS) + slab, BF16),
            pltpu.VMEM((width, cols), BF16),
            pltpu.VMEM((width, 2 * HEAD), BF16),
            pltpu.VMEM((2 * width, HEAD), BF16),
            pltpu.VMEM((cols, width), BF16),
            pltpu.VMEM(kept_rows.shape[2:], jnp.int32),
            pltpu.VMEM(doc_lengths.shape[2:], jnp.int32),
            pltpu.VMEM((3, 2 * HALF_ROWS, width), BF16),
            pltpu.VMEM((5, 2 * HALF_ROWS, width), BF16),
            pltpu.VMEM((3, HALF_ROWS, width), BF16),
            pltpu.VMEM((2 * HALF_ROWS, 2 * HALF_ROWS), BF16),
            pltpu.VMEM((2, 3, 2 * HALF_ROWS, 2 * HEAD), BF16),
            pltpu.VMEM((2, 2, SLABS) + slab, BF16),
            pltpu.VMEM((2, 2, 4) + slab, BF16),
            pltpu.VMEM((2, 2, 4) + slab, BF16),
            pltpu.VMEM((2, 2, 4) + slab, BF16),
            pltpu.VMEM((2, 2) + slab, BF16),
            pltpu.VMEM((2, 2) + slab, BF16),
            pltpu.VMEM((lines, 2 * HEAD), BF16),
        ]
        + [pltpu.VMEM(shape, BF16) for shape in outs]
        + [
            dma((8,)),
            dma((5,)),
            dma((3, 2)),
            dma((3, 2)),
            dma((5, 2, 7)),
            dma((5, 2, SLABS)),
            dma((2, 2)),
            dma((2, 2)),
            dma((2, 2, 3)),
            dma((2, 2, 4)),
            dma((2, 2)),
            dma((2, 2)),
        ],
        compiler_params=pltpu.CompilerParams(
            collective_id=0, has_side_effects=True, vmem_limit_bytes=56 * 1024 * 1024
        ),
        cost_estimate=pl.CostEstimate(flops=4_000_000_000, bytes_accessed=8_000_000, transcendentals=200_000),
        name="section",
    )(
        lines_of(acts_in), lines_of(saved_in), lines_of(out_grad), kept_rows, doc_lengths, w_query,
        w_keyval.reshape(2 * width, HEAD), w_out,
    )
    handed, back, gq, gkv, go = pl.pallas_call(
        copy_kernel,
        out_shape=out_shape,
        in_specs=[anywhere] * 5,
        out_specs=[anywhere] * 5,
        scratch_shapes=[pltpu.VMEM(shape, BF16) for shape in outs] + [dma((5,)), dma((5,))],
        cost_estimate=pl.CostEstimate(flops=0, bytes_accessed=4_000_000, transcendentals=0),
        name="results",
    )(*results)
    return (
        from_lines(handed, acts_in.shape),
        from_lines(back, acts_in.shape),
        gq[None],
        gkv.reshape(1, width // 2, 2, HEAD),
        go[None],
    )


def solution(mesh):
    placed = (
        P("pipe", "dp", None, "tensor", None),
        P("pipe", "dp", None, "tensor", None),
        P("pipe", "dp", None, "tensor", None),
        P("pipe", None, "tensor"),
        P("pipe", None, None, "tensor"),
        P("pipe", "tensor", None),
        P("pipe", "dp", None, None),
        P("pipe", "dp", None, None),
    )
    return jax.shard_map(
        local,
        mesh=mesh,
        in_specs=placed,
        out_specs=(
            P("pipe", "dp", None, "tensor", None),
            P("pipe", "dp", None, "tensor", None),
            P("pipe", "dp", "tensor"),
            P("pipe", "dp", None, "tensor"),
            P("pipe", "tensor", "dp"),
        ),
        check_vma=False,
    )
```
